128 devices in a mesh: seq: 8 (over z_hi, x), tp: 16 (over z_lo, y, core).
Axes of the slice: x: 4, y: 4, z: 4 (z_hi: 2, z_lo: 2; z = z_hi * 2 + z_lo), core: 2. Of those that a mesh axis runs over, the one named last changes fastest.
Arguments:
- rollout_acts: bfloat16 [2048, 8192], P('seq', 'tp'), may hold values from -6 to 6
- rollout_grads: bfloat16 [2048, 8192], P('seq', 'tp'), may hold values from -6 to 6
- lengths: int32 [8, 16], P('seq'), may hold values from 1 to 15, as said below
- destination: int32 [8, 16], P('seq'), may hold values from 0 to 7, as said below
- valid_mask: int32 [2048], P('seq'), may hold values 0 or 1
- advantage: float32 [8, 16], P('seq'), may hold values from -4 to 4
- gate_weight: bfloat16 [8192, 15360], P('tp', 'seq'), may hold values from -0.0625 to 0.0625
- up_weight: bfloat16 [8192, 15360], P('tp', 'seq'), may hold values from -0.0625 to 0.0625
- down_weight: bfloat16 [15360, 8192], P('seq', 'tp'), may hold values from -0.046875 to 0.046875
Outputs:
- block_out: bfloat16 [1024, 8192], P('seq', 'tp')
- input_grad: bfloat16 [1024, 8192], P('seq', 'tp')
- gate_grad: float32 [8192, 15360], P('tp', 'seq')
- up_grad: float32 [8192, 15360], P('tp', 'seq')
- down_grad: float32 [15360, 8192], P('seq', 'tp')
The draws below stay inside these ranges and needn't reach their ends.
Inputs may be any that keep to these rules, and one draw needn't show every extreme that they name: `destination`: in each row every learner shard appears exactly 2 times. The lengths of the responses that one rollout device sends to one learner shard sum to at most 16; in every draw one learner shard receives exactly 16 tokens from every rollout device.
All inputs are finite; a program needn't handle non-finite values. No bound on the sum of `valid_mask` on one device may be relied on, other than what follows from the above.
Results may differ from the reference program's by a relative error of at most 0.0057.
Values may be sent and summed in bfloat16 or wider, within the bound.
A program may use at most 192 MiB of HBM per device.

```python
import jax
import jax.numpy as jnp
from jax import lax

D = 8192
HID = 15360
BIN = 16
RESP = 16
ROLL = 256
LEARN = 128
TOKENS = 1024
N_SEQ = 8


def shuffle_one(order_key):
    return jax.random.permutation(order_key, 2 * N_SEQ)


def routing_plan(key):
    pair_key, cut_key, full_key, long_key, order_key = jax.random.split(key, 5)
    totals = jax.random.randint(pair_key, (N_SEQ, N_SEQ), BIN // 2, BIN + 1)
    full_dest = jax.random.randint(full_key, (), 0, N_SEQ)
    long_source = jax.random.randint(long_key, (), 0, N_SEQ)
    sources = jnp.arange(N_SEQ)[:, None]
    targets = jnp.arange(N_SEQ)[None, :]
    totals = jnp.where(targets == full_dest, BIN, totals)
    cuts = 1 + jax.random.randint(cut_key, (N_SEQ, N_SEQ), 0, BIN) % (totals - 1)
    cuts = jnp.where((sources == long_source) & (targets == full_dest), BIN - 1, cuts)
    pair_lengths = jnp.stack([cuts, totals - cuts], axis=2).reshape(N_SEQ, 2 * N_SEQ)
    orders = jax.vmap(shuffle_one)(jax.random.split(order_key, N_SEQ))
    chosen = jnp.take_along_axis(pair_lengths, orders, axis=1)
    return ((orders // 2).astype(jnp.int32), chosen.astype(jnp.int32))


def draw_lengths(key, part):
    shared = routing_plan(key)
    return shared[1]


def draw_destination(key, part):
    shared = routing_plan(key)
    return shared[0]


def with_ends(array, stream_key, least, largest):
    longest = array.shape.index(max(array.shape))
    spots = []
    for shift in (0, 1):
        where = [jax.random.randint(jax.random.fold_in(stream_key, axis), (), 0, length) for axis, length in enumerate(array.shape)]
        where[longest] = (where[longest] + shift) % array.shape[longest]
        spots.append(tuple(where))
    return array.at[spots[0]].set(least).at[spots[1]].set(largest)


def shard_levels(own_key, dims, pieces, low, largest):
    factor_of = 1.0
    for dim, blocks in pieces:
        draws = jax.random.uniform(jax.random.fold_in(jax.random.fold_in(own_key, 6), dim), (blocks,), jnp.float32, low / len(pieces), largest / len(pieces))
        factor_of = factor_of * jnp.repeat(jnp.exp(draws), dims[dim] // blocks).reshape((-1,) + (1,) * (len(dims) - 1 - dim))
    return factor_of


def noise(stream_key, extent, scale, bound, pieces=(), held_as=jnp.bfloat16):
    factor_of = shard_levels(stream_key, extent, pieces, -0.22, 0.18) if pieces else 1.0
    array = jax.random.normal(stream_key, extent, jnp.float32) * scale * factor_of
    return jnp.minimum(jnp.maximum(array, -bound), bound).astype(held_as)


def setup_inputs(seed: int = 0) -> dict:
    seeds = jax.random.split(jax.random.key(seed), 10)
    return {
        "rollout_acts": noise(seeds[0], (N_SEQ * ROLL, D), 1.0, 6.0, ((0, 8), (1, 16))),
        "rollout_grads": noise(seeds[1], (N_SEQ * ROLL, D), 1.0, 6.0, ((0, 8), (1, 16))),
        "lengths": draw_lengths(jax.random.fold_in(seeds[9], 71), 0),
        "destination": draw_destination(jax.random.fold_in(seeds[9], 71), 0),
        "valid_mask": with_ends((jax.random.randint(seeds[4], (N_SEQ * ROLL,), 0, 4) < 3).astype(jnp.int32), jax.random.fold_in(seeds[4], 1), 0, 1),
        "advantage": noise(seeds[5], (N_SEQ, RESP), 1.0, 4.0, ((0, 8),), jnp.float32),
        "gate_weight": noise(seeds[6], (D, HID), D ** -0.5, 0.0625, ((0, 16), (1, 8))),
        "up_weight": noise(seeds[7], (D, HID), D ** -0.5, 0.0625, ((0, 16), (1, 8))),
        "down_weight": noise(seeds[8], (HID, D), HID ** -0.5, 0.046875, ((0, 8), (1, 16))),
    }


def place_rows(lengths, destination):
    order = jnp.arange(RESP)
    same = destination[:, :, None] == destination[:, None, :]
    earlier = order[None, :] < order[:, None]
    offsets = lax.optimization_barrier(jnp.sum(jnp.where(same & earlier[None], lengths[:, None, :], 0), axis=2))
    within = jnp.arange(BIN)
    sources = jnp.arange(N_SEQ)
    target = destination[:, :, None] * LEARN + sources[:, None, None] * BIN + offsets[:, :, None] + within[None, None, :]
    live = within[None, None, :] < lengths[:, :, None]
    target = jnp.where(live, target, TOKENS)
    return target.reshape(-1).astype(jnp.int32)

def pack_rows(rows, target):
    holder = jnp.zeros((TOKENS + 1, rows.shape[1]), rows.dtype)
    return holder.at[target].set(rows)[:TOKENS]

def reference(rollout_acts, rollout_grads, lengths, destination, valid_mask, advantage, gate_weight, up_weight, down_weight):
    target = place_rows(lengths, destination)
    row_weight = jnp.repeat(advantage.reshape(-1), BIN) * valid_mask.astype(jnp.float32)
    scaled = (rollout_grads.astype(jnp.float32) * row_weight[:, None]).astype(jnp.bfloat16)
    learner_acts = pack_rows(rollout_acts, target)
    learner_grads = pack_rows(scaled, target)
    paired = jnp.concatenate([gate_weight, up_weight], axis=1)
    gate_up = jnp.dot(learner_acts, paired, preferred_element_type=jnp.float32)
    gate = gate_up[:, :HID]
    upper = gate_up[:, HID:]
    sigma = jax.nn.sigmoid(gate)
    hidden = (gate * sigma * upper).astype(jnp.bfloat16)
    block_out = jnp.dot(hidden, down_weight, preferred_element_type=jnp.float32).astype(jnp.bfloat16)
    grad_hidden = jnp.dot(learner_grads, down_weight.T, preferred_element_type=jnp.float32)
    grad_gate = grad_hidden * upper * sigma * (1.0 + gate * (1.0 - sigma))
    grad_upper = grad_hidden * gate * sigma
    grad_pre = jnp.concatenate([grad_gate, grad_upper], axis=1).astype(jnp.bfloat16)
    input_grad = jnp.dot(grad_pre, paired.T, preferred_element_type=jnp.float32).astype(jnp.bfloat16)
    grad_scale = 1.0 / jnp.sqrt(jnp.float32(TOKENS))
    pair_grad = jnp.dot(learner_acts.T, grad_pre, preferred_element_type=jnp.float32) * grad_scale
    down_grad = jnp.dot(hidden.T, learner_grads, preferred_element_type=jnp.float32) * grad_scale
    return (block_out, input_grad, pair_grad[:, :HID], pair_grad[:, HID:], down_grad)
```

```python
import jax
import jax.numpy as jnp
from jax import lax
from jax.experimental import pallas as pl
from jax.experimental.pallas import tpu as pltpu
from jax.sharding import PartitionSpec as P

BIN = 16
NC = 4
WIDTH = 512
HID = 1920
ALL = 3 * HID
CY = 3200
CZ = ALL - CY
HZ = CZ // 2
UNIT = 640
BF = jnp.bfloat16
F32 = jnp.float32
MESH = pl.DeviceIdType.MESH

SEQ_NAMES = ["zh", "xo+", "xo-", "xp+", "xp-", "xf+", "xf-"]
W_NAMES = ["wg", "wu", "wd"]
CHUNK_NAMES = [
    "q",
    "y1+", "y1-", "yo+", "yo-", "ya+", "ya-", "yz",
    "z1", "r1+", "r1-", "ro+", "ro-", "ra+", "ra-",
    "az", "ay+", "ay-", "by+", "by-", "bz0", "ap+", "ap-", "bf+", "bf-",
    "bz1", "bz2", "af+", "af-", "bz3", "core",
]
SEM = {}
for _n in SEQ_NAMES + W_NAMES:
    SEM[(_n, 0)] = len(SEM)
for _k in range(NC):
    for _n in CHUNK_NAMES:
        SEM[(_n, _k)] = len(SEM)
N_SEM = len(SEM)

YCOL = pl.ds(0, CY)
ZCOL = pl.ds(CY, CZ)
ZCOL_A = pl.ds(CY, HZ)
ZCOL_B = pl.ds(CY + HZ, HZ)


def up32(value):
    return value.astype(F32)


def mega(
    acts_ref, grads_ref, hot_ref, weight_ref, gate_hbm, up_hbm, down_hbm,
    hid_out, gg_out, gu_out, acts_out, grads_out,
    wg, wu, wd, pg, pu, pd, G, Q, PP, H,
    y1, yown, yacc, ysend, yz, z1, r1, rown, racc, F,
    ssem, rsem, lsem,
):
    s = lax.axis_index("seq")
    t = lax.axis_index("tp")
    zh, x = s // 4, lax.rem(s, 4)
    zl, y, c = t // 8, lax.rem(t // 2, 4), lax.rem(t, 2)
    oz, oc, oh = 1 - zl, 1 - c, 1 - zh
    yp, ym, y2 = lax.rem(y + 1, 4), lax.rem(y + 3, 4), lax.rem(y + 2, 4)

    def dev(zh_=zh, x_=x, zl_=zl, y_=y, c_=c):
        return (zh_ * 4 + x_, zl_ * 8 + y_ * 2 + c_)

    XP, XM = dev(x_=lax.rem(x + 1, 4)), dev(x_=lax.rem(x + 3, 4))
    YP, YM = dev(y_=yp), dev(y_=ym)
    ZL, ZH, CO = dev(zl_=oz), dev(zh_=oh), dev(c_=oc)

    copies = {}

    def send(name, k, src, dst, to):
        i = SEM[(name, k)]
        cp = pltpu.make_async_remote_copy(
            src_ref=src, dst_ref=dst, send_sem=ssem.at[i], recv_sem=rsem.at[i],
            device_id=to, device_id_type=MESH,
        )
        cp.start()
        copies[(name, k)] = cp

    def recv(name, k):
        copies[(name, k)].wait_recv()

    local = []

    def local_copy(src, dst):
        cp = pltpu.make_async_copy(src, dst, lsem.at[len(local)])
        cp.start()
        local.append(cp)
        return cp

    loads = [local_copy(gate_hbm, wg), local_copy(up_hbm, wu), local_copy(down_hbm, wd)]
    barrier = pltpu.get_barrier_semaphore()
    for peer in (XP, XM, YP, YM, ZL, ZH, CO):
        pl.semaphore_signal(barrier, inc=1, device_id=peer, device_id_type=MESH)

    hot = hot_ref[...]
    G[0, 0, zh] = jnp.dot(hot, acts_ref[...], preferred_element_type=F32).astype(BF)
    scaled = (up32(grads_ref[...]) * weight_ref[...]).astype(BF)
    G[1, 0, zh] = jnp.dot(hot, scaled, preferred_element_type=F32).astype(BF)

    pl.semaphore_wait(barrier, 7)

    send("zh", 0, G.at[:, 0, zh], G.at[:, 0, zh], ZH)
    send("xo+", 0, G.at[:, 0, zh], G.at[:, 1, zh], XP)
    send("xo-", 0, G.at[:, 0, zh], G.at[:, 2, zh], XM)
    for cp, name, src, dst in zip(loads, W_NAMES, (wg, wu, wd), (pg, pu, pd)):
        cp.wait()
        send(name, 0, src, dst, CO)
    recv("zh", 0)
    send("q", 0, G.at[:, 0, oc], Q.at[:, 0], CO)
    send("xp+", 0, G.at[:, 0, oh], G.at[:, 1, oh], XP)
    send("xp-", 0, G.at[:, 0, oh], G.at[:, 2, oh], XM)

    def forward(k):
        recv("q", k)
        a_own, a_par = G[0, k, c], Q[0, k]
        for own, par, first in ((wg, pg, 0), (wu, pu, HID)):
            def unit(u, carry, own=own, par=par, first=first):
                cols = pl.ds(pl.multiple_of(u * UNIT, 128), UNIT)
                to = pl.ds(pl.multiple_of(u * UNIT + first, 128), UNIT)
                part = jnp.dot(a_own, own[:, cols], preferred_element_type=F32)
                part += jnp.dot(a_par, par[:, cols], preferred_element_type=F32)
                PP[k, :, :, to] = part.astype(BF).reshape(8, BIN, UNIT)
                return carry
            lax.fori_loop(0, 3, unit, 0)
        send("y1+", k, PP.at[k, y2, :, YCOL], y1.at[k, 0], YP)
        send("y1-", k, PP.at[k, 4 + y2, :, YCOL], y1.at[k, 1], YM)
        send("yo+", k, PP.at[k, 4 + yp, :, YCOL], yown.at[k, 1], YP)
        send("yo-", k, PP.at[k, ym, :, YCOL], yown.at[k, 0], YM)
        g_own, g_par = G[1, k, c], Q[1, k]

        def unit_back(u, carry):
            rows = pl.ds(pl.multiple_of(u * UNIT, 128), UNIT)
            to = pl.ds(pl.multiple_of(u * UNIT + 2 * HID, 128), UNIT)
            nt = (((1,), (1,)), ((), ()))
            part = lax.dot_general(g_own, wd[rows, :], nt, preferred_element_type=F32)
            part += lax.dot_general(g_par, pd[rows, :], nt, preferred_element_type=F32)
            PP[k, :, :, to] = part.astype(BF).reshape(8, BIN, UNIT)
            return carry
        lax.fori_loop(0, 3, unit_back, 0)
        send("z1", k, PP.at[k, pl.ds(oz * 4, 4), :, ZCOL], z1.at[k], ZL)

    def reduce_one(k):
        recv("y1+", k)
        y1[k, 0] = (up32(y1[k, 0]) + up32(PP[k, yp, :, YCOL])).astype(BF)
        send("ya+", k, y1.at[k, 0], yacc.at[k, 0], YP)
        recv("y1-", k)
        y1[k, 1] = (up32(y1[k, 1]) + up32(PP[k, 4 + ym, :, YCOL])).astype(BF)
        send("ya-", k, y1.at[k, 1], yacc.at[k, 1], YM)
        recv("z1", k)
        for row in (y2, yp, ym):
            z1[k, row] = (up32(z1[k, row]) + up32(PP[k, zl * 4 + row, :, ZCOL])).astype(BF)
        send("r1+", k, z1.at[k, y2, :, pl.ds(0, HZ)], r1.at[k, 0], YP)
        send("r1-", k, z1.at[k, y2, :, pl.ds(HZ, HZ)], r1.at[k, 1], YM)
        send("ro+", k, z1.at[k, yp, :, pl.ds(HZ, HZ)], rown.at[k, 1], YP)
        send("ro-", k, z1.at[k, ym, :, pl.ds(0, HZ)], rown.at[k, 0], YM)

    def reduce_two(k):
        for name in ("yo+", "yo-", "ya+", "ya-"):
            recv(name, k)
        ysend[k] = (
            up32(PP[k, oz * 4 + y, :, YCOL]) + up32(yacc[k, oz]) + up32(yown[k, oz])
        ).astype(BF)
        send("yz", k, ysend.at[k], yz.at[k], ZL)
        recv("r1+", k)
        r1[k, 0] = (up32(r1[k, 0]) + up32(z1[k, yp, :, pl.ds(0, HZ)])).astype(BF)
        send("ra+", k, r1.at[k, 0], racc.at[k, 0], YP)
        recv("r1-", k)
        r1[k, 1] = (up32(r1[k, 1]) + up32(z1[k, ym, :, pl.ds(HZ, HZ)])).astype(BF)
        send("ra-", k, r1.at[k, 1], racc.at[k, 1], YM)

    def finish(k):
        for name in ("yz", "ro+", "ro-", "ra+", "ra-"):
            recv(name, k)
        mine = zl * 4 + y
        F[:, YCOL] = (
            up32(PP[k, mine, :, YCOL]) + up32(yacc[k, zl]) + up32(yown[k, zl]) + up32(yz[k])
        )
        for half, cols in ((0, ZCOL_A), (1, ZCOL_B)):
            F[:, cols] = (
                up32(PP[k, mine, :, cols]) + up32(z1[k, y, :, pl.ds(half * HZ, HZ)])
                + up32(racc[k, half]) + up32(rown[k, half])
            )
        gate, upper, back = F[:, :HID], F[:, HID:2 * HID], F[:, 2 * HID:]
        sigma = jax.nn.sigmoid(gate)
        swish = gate * sigma
        H[k, c, mine, :, :HID] = (swish * upper).astype(BF)
        H[k, c, mine, :, HID:2 * HID] = (
            back * upper * sigma * (1.0 + gate * (1.0 - sigma))
        ).astype(BF)
        H[k, c, mine, :, 2 * HID:] = (back * swish).astype(BF)
        a = H.at[k, c, mine, :, YCOL]
        b = H.at[k, c, mine, :, ZCOL]
        send("az", k, a, a, ZL)
        send("ay+", k, a, a, YP)
        send("ay-", k, a, a, YM)
        send("by+", k, b, b, YP)
        send("by-", k, b, b, YM)
        send("bz0", k, b, b, ZL)

    def gather_one(k):
        recv("by+", k)
        b = H.at[k, c, zl * 4 + ym, :, ZCOL_A]
        send("bf+", k, b, b, YP)
        b = H.at[k, c, zl * 4 + ym, :, ZCOL]
        send("bz1", k, b, b, ZL)
        recv("by-", k)
        b = H.at[k, c, zl * 4 + yp, :, ZCOL_B]
        send("bf-", k, b, b, YM)
        b = H.at[k, c, zl * 4 + yp, :, ZCOL]
        send("bz2", k, b, b, ZL)
        recv("az", k)
        a = H.at[k, c, oz * 4 + y, :, YCOL]
        send("ap+", k, a, a, YP)
        send("ap-", k, a, a, YM)
        recv("ay+", k)
        a = H.at[k, c, zl * 4 + ym, :, YCOL]
        send("af+", k, a, a, YP)
        recv("ay-", k)

    def gather_two(k):
        recv("bf+", k)
        recv("bf-", k)
        b = H.at[k, c, zl * 4 + y2, :, ZCOL]
        send("bz3", k, b, b, ZL)
        recv("ap+", k)
        recv("ap-", k)
        a = H.at[k, c, oz * 4 + yp, :, YCOL]
        send("af-", k, a, a, YM)

    def gather_three(k):
        for name in ("af+", "af-", "bz0", "bz1", "bz2", "bz3"):
            recv(name, k)
        send("core", k, H.at[k, c], H.at[k, c], CO)

    def last(k):
        recv("core", k)
        for first, out in ((0, hid_out), (HID, gg_out), (2 * HID, gu_out)):
            local_copy(H.at[k, :, :, :, pl.ds(first, HID)], out.at[k])

    def seq_one():
        for name in ("xo+", "xp+", "xo-", "xp-"):
            recv(name, 0)
        send("xf+", 0, G.at[:, 1, 0], G.at[:, 3, 0], XP)
        send("xf-", 0, G.at[:, 2, 1], G.at[:, 3, 1], XM)
        send("q", 1, G.at[:, 1, oc], Q.at[:, 1], CO)
        send("q", 2, G.at[:, 2, oc], Q.at[:, 2], CO)

    def seq_two():
        recv("xf+", 0)
        recv("xf-", 0)
        send("q", 3, G.at[:, 3, oc], Q.at[:, 3], CO)
        local_copy(G.at[0], acts_out)
        local_copy(G.at[1], grads_out)

    for name in W_NAMES:
        recv(name, 0)
    stages = [forward, reduce_one, reduce_two, finish, gather_one, gather_two, gather_three, last]
    for slot in range(NC + len(stages) - 1):
        if slot < NC:
            forward(slot)
        if slot == 0:
            seq_one()
        if slot == 2:
            seq_two()
        for k in range(NC):
            stage = slot - k
            if 1 <= stage < len(stages):
                stages[stage](k)
    for cp in copies.values():
        cp.wait_send()
    for cp in local[len(loads):]:
        cp.wait()


def run_mega(acts, grads, hot, weight, gate, up, down):
    vm = pltpu.VMEM
    shape = jax.ShapeDtypeStruct
    rows = shape((NC, 2, 8, BIN, HID), BF)
    packed = shape((NC, 2, 128, WIDTH), BF)
    return pl.pallas_call(
        mega,
        out_shape=(rows, rows, rows, packed, packed),
        in_specs=[pl.BlockSpec(memory_space=vm)] * 4 + [pl.BlockSpec(memory_space=pl.ANY)] * 3,
        out_specs=tuple([pl.BlockSpec(memory_space=pl.ANY)] * 5),
        scratch_shapes=[
            vm((WIDTH, HID), BF), vm((WIDTH, HID), BF), vm((HID, WIDTH), BF),
            vm((WIDTH, HID), BF), vm((WIDTH, HID), BF), vm((HID, WIDTH), BF),
            vm((2, NC, 2, 128, WIDTH), BF),
            vm((2, NC, 128, WIDTH), BF),
            vm((NC, 8, BIN, ALL), BF),
            vm((NC, 2, 8, BIN, ALL), BF),
            vm((NC, 2, BIN, CY), BF), vm((NC, 2, BIN, CY), BF), vm((NC, 2, BIN, CY), BF),
            vm((NC, BIN, CY), BF), vm((NC, BIN, CY), BF),
            vm((NC, 4, BIN, CZ), BF),
            vm((NC, 2, BIN, HZ), BF), vm((NC, 2, BIN, HZ), BF), vm((NC, 2, BIN, HZ), BF),
            vm((BIN, ALL), F32),
            pltpu.SemaphoreType.DMA((N_SEM,)),
            pltpu.SemaphoreType.DMA((N_SEM,)),
            pltpu.SemaphoreType.DMA((32,)),
        ],
        compiler_params=pltpu.CompilerParams(
            collective_id=0, has_side_effects=True, vmem_limit_bytes=60 * 2**20
        ),
        name="mega",
    )(acts, grads, hot, weight, gate, up, down)


def per_device(
    rollout_acts, rollout_grads, lengths, destination, valid_mask, advantage,
    gate_weight, up_weight, down_weight,
):
    x = lax.rem(lax.axis_index("seq"), 4)
    own_lengths = lengths[0]
    own_dest = destination[0]
    order = jnp.arange(own_dest.shape[0])
    same = own_dest[:, None] == own_dest[None, :]
    earlier = order[None, :] < order[:, None]
    offsets = jnp.sum(jnp.where(same & earlier, own_lengths[None, :], 0), axis=1)
    within = jnp.arange(BIN)
    target = own_dest[:, None] * BIN + offsets[:, None] + within[None, :]
    live = within[None, :] < own_lengths[:, None]
    target = jnp.where(live, target, -1).reshape(-1)
    hot = (jnp.arange(8 * BIN)[:, None] == target[None, :]).astype(BF)
    row_weight = jnp.repeat(advantage[0], BIN) * valid_mask.astype(F32)
    hidden, gg, gu, acts, grads = run_mega(
        rollout_acts, rollout_grads, hot, row_weight[:, None], gate_weight, up_weight, down_weight
    )
    total = 1024
    hidden, gg, gu = (v.reshape(total, HID) for v in (hidden, gg, gu))
    acts, grads = acts.reshape(total, WIDTH), grads.reshape(total, WIDTH)
    block = jnp.dot(hidden, down_weight, preferred_element_type=F32)
    nt = (((1,), (1,)), ((), ()))
    inner = lax.dot_general(gg, gate_weight, nt, preferred_element_type=F32)
    inner += lax.dot_general(gu, up_weight, nt, preferred_element_type=F32)
    both = jnp.concatenate([block, inner], axis=1).reshape(NC, 2, 8, BIN, 2 * WIDTH)
    chunk_of = jnp.array([0, 2, 3, 1])[lax.rem(jnp.arange(4) - x + 4, 4)]
    both = both[chunk_of]
    both = both.transpose(2, 1, 0, 3, 4).reshape(total, 2 * WIDTH)
    both = lax.psum_scatter(both, "seq", scatter_dimension=0, tiled=True).astype(BF)
    scale = 1.0 / jnp.sqrt(jnp.float32(total))
    tn = (((0,), (0,)), ((), ()))
    gate_grad = lax.dot_general(acts, gg, tn, preferred_element_type=F32) * scale
    up_grad = lax.dot_general(acts, gu, tn, preferred_element_type=F32) * scale
    down_grad = lax.dot_general(hidden, grads, tn, preferred_element_type=F32) * scale
    return both[:, :WIDTH], both[:, WIDTH:], gate_grad, up_grad, down_grad


def solution(mesh):
    return jax.shard_map(
        per_device,
        mesh=mesh,
        in_specs=(
            P("seq", "tp"), P("seq", "tp"), P("seq", None), P("seq", None), P("seq"),
            P("seq", None), P("tp", "seq"), P("tp", "seq"), P("seq", "tp"),
        ),
        out_specs=(P("seq", "tp"), P("seq", "tp"), P("tp", "seq"), P("tp", "seq"), P("seq", "tp")),
        check_vma=False,
    )
```

```python
import jax
import jax.numpy as jnp
from jax import lax
from jax.experimental import pallas as pl
from jax.experimental.pallas import tpu as pltpu
from jax.sharding import PartitionSpec as P

BIN = 16
NC = 4
WIDTH = 512
HID = 1920
ALL = 3 * HID
CY = 3456
CZ = ALL - CY
HZ = CZ // 2
UNIT = 640
BF = jnp.bfloat16
F32 = jnp.float32
MESH = pl.DeviceIdType.MESH

SEQ_NAMES = [
    "zha", "zhg", "xoa+", "xoa-", "xog+", "xog-", "xpa+", "xpa-", "xpg+", "xpg-", "xf+", "xf-",
    "sz", "dx+", "dx-", "dx2", "dz", "dzx+", "dzx-", "dzx2",
]
W_NAMES = ["wg", "wu", "wd"]
CHUNK_NAMES = [
    "qa", "qg",
    "y1+", "y1-", "yo+", "yo-", "ya+", "ya-", "yz",
    "z1", "r1+", "r1-", "ro+", "ro-", "ra+", "ra-",
    "az", "ay+", "ay-", "by+", "by-", "bz0", "ap+", "ap-", "bf+", "bf-",
    "bz1", "bz2", "af+", "af-", "bz3", "core",
    "m+", "m-", "m2",
]
SEM = {}
for _n in SEQ_NAMES + W_NAMES:
    SEM[(_n, 0)] = len(SEM)
for _k in range(NC):
    for _n in CHUNK_NAMES:
        SEM[(_n, _k)] = len(SEM)
N_SEM = len(SEM)

YCOL = pl.ds(0, CY)
ZCOL = pl.ds(CY, CZ)
ZCOL_A = pl.ds(CY, HZ)
ZCOL_B = pl.ds(CY + HZ, HZ)


def up32(value):
    return value.astype(F32)


def routing(lengths, destination, advantage, mask):
    diagonal = lax.broadcasted_iota(jnp.int32, (16, 16), 0) == lax.broadcasted_iota(jnp.int32, (16, 16), 1)

    def column(row):
        return jnp.sum(jnp.where(diagonal, row, jnp.zeros_like(row)), axis=1, keepdims=True)

    resp = lax.broadcasted_iota(jnp.int32, (16, 256), 0)
    row = lax.broadcasted_iota(jnp.int32, (16, 256), 1)
    of_row = row // BIN
    mine = of_row == resp

    def spread(col):
        return jnp.sum(jnp.where(mine, col, jnp.zeros_like(col)), axis=0, keepdims=True)

    len_col, dest_col = column(lengths), column(destination)
    len_row, dest_row = spread(len_col), spread(dest_col)
    before = (dest_col == dest_row) & (resp < of_row)
    offset = jnp.sum(jnp.where(before, len_col, 0), axis=0, keepdims=True)
    within = lax.rem(row[:1], BIN)
    slot = jnp.where(within < len_row, dest_row * BIN + offset + within, -1)
    hot = lax.broadcasted_iota(jnp.int32, (128, 256), 0) == slot
    weight = spread(column(advantage)) * mask.astype(F32)
    weight = jnp.sum(jnp.where(hot, weight, 0.0), axis=1, keepdims=True)
    return jnp.where(hot, 1.0, 0.0).astype(BF), weight


def mega(
    acts_ref, grads_ref, lengths_ref, dest_ref, mask_ref, adv_ref, gate_hbm, up_hbm, down_hbm,
    block_out, input_out, gate_out, up_out, down_out,
    wg, wu, wd, pg, pu, pd, G, Q, PP, H,
    y1, yown, yacc, ysend, yz, z1, r1, rown, racc, F,
    OB, OL, rm, rp, r2, sz, rz, dr, tg, tu, td,
    ssem, rsem, lsem,
):
    s = lax.axis_index("seq")
    t = lax.axis_index("tp")
    zh, x = s // 4, lax.rem(s, 4)
    zl, y, c = t // 8, lax.rem(t // 2, 4), lax.rem(t, 2)
    oz, oc, oh = 1 - zl, 1 - c, 1 - zh
    yp, ym, y2 = lax.rem(y + 1, 4), lax.rem(y + 3, 4), lax.rem(y + 2, 4)

    def dev(zh_=zh, x_=x, zl_=zl, y_=y, c_=c):
        return (zh_ * 4 + x_, zl_ * 8 + y_ * 2 + c_)

    XP, XM = dev(x_=lax.rem(x + 1, 4)), dev(x_=lax.rem(x + 3, 4))
    YP, YM = dev(y_=yp), dev(y_=ym)
    xp, xm, x2 = lax.rem(x + 1, 4), lax.rem(x + 3, 4), lax.rem(x + 2, 4)
    ZL, ZH, CO = dev(zl_=oz), dev(zh_=oh), dev(c_=oc)

    copies = {}

    def send(name, k, src, dst, to):
        i = SEM[(name, k)]
        cp = pltpu.make_async_remote_copy(
            src_ref=src, dst_ref=dst, send_sem=ssem.at[i], recv_sem=rsem.at[i],
            device_id=to, device_id_type=MESH,
        )
        cp.start()
        copies[(name, k)] = cp

    def recv(name, k):
        copies[(name, k)].wait_recv()

    local = []

    def local_copy(src, dst):
        cp = pltpu.make_async_copy(src, dst, lsem.at[len(local)])
        cp.start()
        local.append(cp)
        return cp

    loads = [local_copy(gate_hbm, wg), local_copy(up_hbm, wu), local_copy(down_hbm, wd)]
    barrier = pltpu.get_barrier_semaphore()
    peers = [XP, XM, YP, YM, ZL, ZH, CO, dev(x_=x2)]
    peers += [dev(zh_=oh, x_=x_) for x_ in (xp, xm, x2)]
    for peer in peers:
        pl.semaphore_signal(barrier, inc=1, device_id=peer, device_id_type=MESH)

    hot, weight = routing(lengths_ref[...], dest_ref[...], adv_ref[...], mask_ref[...])
    G[0, 0, zh] = jnp.dot(hot, acts_ref[...], preferred_element_type=F32).astype(BF)
    pl.semaphore_wait(barrier, len(peers))
    for arr, n in ((0, "a"), (1, "g")):
        if arr == 1:
            packed = jnp.dot(hot, grads_ref[...], preferred_element_type=F32)
            G[1, 0, zh] = (packed * weight).astype(BF)
        send("zh" + n, 0, G.at[arr, 0, zh], G.at[arr, 0, zh], ZH)
        send("xo" + n + "+", 0, G.at[arr, 0, zh], G.at[arr, 1, zh], XP)
        send("xo" + n + "-", 0, G.at[arr, 0, zh], G.at[arr, 2, zh], XM)
    for cp, name, src, dst in zip(loads, W_NAMES, (wg, wu, wd), (pg, pu, pd)):
        cp.wait()
        send(name, 0, src, dst, CO)
    for arr, n in ((0, "a"), (1, "g")):
        recv("zh" + n, 0)
        send("q" + n, 0, G.at[arr, 0, oc], Q.at[arr, 0], CO)
        send("xp" + n + "+", 0, G.at[arr, 0, oh], G.at[arr, 1, oh], XP)
        send("xp" + n + "-", 0, G.at[arr, 0, oh], G.at[arr, 2, oh], XM)

    def forward(k):
        recv("qa", k)
        a_own, a_par = G[0, k, c], Q[0, k]
        for own, par, first, name in ((wg, pg, 0, "wg"), (wu, pu, HID, "wu")):
            if k == 0:
                recv(name, 0)

            def unit(u, carry, own=own, par=par, first=first):
                cols = pl.ds(pl.multiple_of(u * UNIT, 128), UNIT)
                to = pl.ds(pl.multiple_of(u * UNIT + first, 128), UNIT)
                part = jnp.dot(a_own, own[:, cols], preferred_element_type=F32)
                part += jnp.dot(a_par, par[:, cols], preferred_element_type=F32)
                PP[k, :, :, to] = part.astype(BF).reshape(8, BIN, UNIT)
                return carry
            lax.fori_loop(0, 3, unit, 0)
        send("y1+", k, PP.at[k, y2, :, YCOL], y1.at[k, 0], YP)
        send("y1-", k, PP.at[k, 4 + y2, :, YCOL], y1.at[k, 1], YM)
        send("yo+", k, PP.at[k, 4 + yp, :, YCOL], yown.at[k, 1], YP)
        send("yo-", k, PP.at[k, ym, :, YCOL], yown.at[k, 0], YM)
        recv("qg", k)
        if k == 0:
            recv("wd", 0)
        g_own, g_par = G[1, k, c], Q[1, k]

        def unit_back(u, carry):
            rows = pl.ds(pl.multiple_of(u * UNIT, 128), UNIT)
            to = pl.ds(pl.multiple_of(u * UNIT + 2 * HID, 128), UNIT)
            nt = (((1,), (1,)), ((), ()))
            part = lax.dot_general(g_own, wd[rows, :], nt, preferred_element_type=F32)
            part += lax.dot_general(g_par, pd[rows, :], nt, preferred_element_type=F32)
            PP[k, :, :, to] = part.astype(BF).reshape(8, BIN, UNIT)
            return carry
        lax.fori_loop(0, 3, unit_back, 0)
        send("z1", k, PP.at[k, pl.ds(oz * 4, 4), :, ZCOL], z1.at[k], ZL)

    def reduce_one(k):
        recv("y1+", k)
        y1[k, 0] = (up32(y1[k, 0]) + up32(PP[k, yp, :, YCOL])).astype(BF)
        send("ya+", k, y1.at[k, 0], yacc.at[k, 0], YP)
        recv("y1-", k)
        y1[k, 1] = (up32(y1[k, 1]) + up32(PP[k, 4 + ym, :, YCOL])).astype(BF)
        send("ya-", k, y1.at[k, 1], yacc.at[k, 1], YM)
        recv("z1", k)
        for row in (y2, yp, ym):
            z1[k, row] = (up32(z1[k, row]) + up32(PP[k, zl * 4 + row, :, ZCOL])).astype(BF)
        send("r1+", k, z1.at[k, y2, :, pl.ds(0, HZ)], r1.at[k, 0], YP)
        send("r1-", k, z1.at[k, y2, :, pl.ds(HZ, HZ)], r1.at[k, 1], YM)
        send("ro+", k, z1.at[k, yp, :, pl.ds(HZ, HZ)], rown.at[k, 1], YP)
        send("ro-", k, z1.at[k, ym, :, pl.ds(0, HZ)], rown.at[k, 0], YM)

    def reduce_two(k):
        for name in ("yo+", "yo-", "ya+", "ya-"):
            recv(name, k)
        ysend[k] = (
            up32(PP[k, oz * 4 + y, :, YCOL]) + up32(yacc[k, oz]) + up32(yown[k, oz])
        ).astype(BF)
        send("yz", k, ysend.at[k], yz.at[k], ZL)
        recv("r1+", k)
        r1[k, 0] = (up32(r1[k, 0]) + up32(z1[k, yp, :, pl.ds(0, HZ)])).astype(BF)
        send("ra+", k, r1.at[k, 0], racc.at[k, 0], YP)
        recv("r1-", k)
        r1[k, 1] = (up32(r1[k, 1]) + up32(z1[k, ym, :, pl.ds(HZ, HZ)])).astype(BF)
        send("ra-", k, r1.at[k, 1], racc.at[k, 1], YM)

    def finish(k):
        for name in ("yz", "ro+", "ro-", "ra+", "ra-"):
            recv(name, k)
        mine = zl * 4 + y
        F[:, YCOL] = (
            up32(PP[k, mine, :, YCOL]) + up32(yacc[k, zl]) + up32(yown[k, zl]) + up32(yz[k])
        )
        for half, cols in ((0, ZCOL_A), (1, ZCOL_B)):
            F[:, cols] = (
                up32(PP[k, mine, :, cols]) + up32(z1[k, y, :, pl.ds(half * HZ, HZ)])
                + up32(racc[k, half]) + up32(rown[k, half])
            )
        gate, upper, back = F[:, :HID], F[:, HID:2 * HID], F[:, 2 * HID:]
        sigma = jax.nn.sigmoid(gate)
        swish = gate * sigma
        H[k, c, mine, :, :HID] = (swish * upper).astype(BF)
        H[k, c, mine, :, HID:2 * HID] = (
            back * upper * sigma * (1.0 + gate * (1.0 - sigma))
        ).astype(BF)
        H[k, c, mine, :, 2 * HID:] = (back * swish).astype(BF)
        a = H.at[k, c, mine, :, YCOL]
        b = H.at[k, c, mine, :, ZCOL]
        send("az", k, a, a, ZL)
        send("ay+", k, a, a, YP)
        send("ay-", k, a, a, YM)
        send("by+", k, b, b, YP)
        send("by-", k, b, b, YM)
        send("bz0", k, b, b, ZL)

    def gather_one(k):
        recv("by+", k)
        b = H.at[k, c, zl * 4 + ym, :, ZCOL_A]
        send("bf+", k, b, b, YP)
        b = H.at[k, c, zl * 4 + ym, :, ZCOL]
        send("bz1", k, b, b, ZL)
        recv("by-", k)
        b = H.at[k, c, zl * 4 + yp, :, ZCOL_B]
        send("bf-", k, b, b, YM)
        b = H.at[k, c, zl * 4 + yp, :, ZCOL]
        send("bz2", k, b, b, ZL)
        recv("az", k)
        a = H.at[k, c, oz * 4 + y, :, YCOL]
        send("ap+", k, a, a, YP)
        send("ap-", k, a, a, YM)
        recv("ay+", k)
        a = H.at[k, c, zl * 4 + ym, :, YCOL]
        send("af+", k, a, a, YP)
        recv("ay-", k)

    def gather_two(k):
        recv("bf+", k)
        recv("bf-", k)
        b = H.at[k, c, zl * 4 + y2, :, ZCOL]
        send("bz3", k, b, b, ZL)
        recv("ap+", k)
        recv("ap-", k)
        a = H.at[k, c, oz * 4 + yp, :, YCOL]
        send("af-", k, a, a, YM)

    def gather_three(k):
        for name in ("af+", "af-", "bz0", "bz1", "bz2", "bz3"):
            recv(name, k)
        send("core", k, H.at[k, c], H.at[k, c], CO)

    def last(k):
        recv("core", k)
        nt = (((1,), (1,)), ((), ()))
        shape = (2, 2, 4, BIN, WIDTH)
        h = H[k, :, :, :, :HID].reshape(256, HID)
        part = jnp.dot(h, wd[...], preferred_element_type=F32).reshape(shape)
        OB[k, :, :, :, :, :WIDTH] = part
        if k == NC - 1:
            OL[:, :, :, :, :WIDTH] = part.astype(BF)
        h = H[k, :, :, :, HID:2 * HID].reshape(256, HID)
        part = lax.dot_general(h, wg[...], nt, preferred_element_type=F32)
        h = H[k, :, :, :, 2 * HID:].reshape(256, HID)
        part += lax.dot_general(h, wu[...], nt, preferred_element_type=F32)
        part = part.reshape(shape)
        OB[k, :, :, :, :, WIDTH:] = part
        if k < NC - 1:
            send("m+", k, OB.at[k, :, :, xp], rm.at[k], XP)
            send("m-", k, OB.at[k, :, :, xm], rp.at[k], XM)
            send("m2", k, OB.at[k, :, :, x2], r2.at[k], dev(x_=x2))
        else:
            OL[:, :, :, :, WIDTH:] = part.astype(BF)
            send("dzx2", 0, OL.at[:, oh, x2], dr.at[6], dev(zh_=oh, x_=x2))
            send("dzx+", 0, OL.at[:, oh, xp], dr.at[4], dev(zh_=oh, x_=xp))
            send("dzx-", 0, OL.at[:, oh, xm], dr.at[5], dev(zh_=oh, x_=xm))
            send("dz", 0, OL.at[:, oh, x], dr.at[3], ZH)
            send("dx2", 0, OL.at[:, zh, x2], dr.at[2], dev(x_=x2))
            send("dx+", 0, OL.at[:, zh, xp], dr.at[0], XP)
            send("dx-", 0, OL.at[:, zh, xm], dr.at[1], XM)

    PLACES = ((0, 2, 1, 3), (2, 3, 0, 1), (3, 1, 2, 0), (1, 0, 3, 2))

    def earlier_sum(r, half):
        total = None
        for k, ref in zip(PLACES[r], (None, rm, rp, r2)):
            if k < NC - 1:
                part = OB[k, :, half, x] if ref is None else ref[k, :, half]
                total = part if total is None else total + part
        return total

    def seq_exchange():
        for k in range(NC - 1):
            for name in ("m+", "m-", "m2"):
                recv(name, k)
        for r in range(4):
            sz[r] = earlier_sum(r, oh).astype(BF)
        send("sz", 0, sz, rz, ZH)

    def seq_finish():
        for name in ("dx+", "dx-", "dx2", "dz", "dzx+", "dzx-", "dzx2", "sz"):
            recv(name, 0)
        late = {0: (2, 6), 1: (0, 4), 2: (3,), 3: (1, 5)}
        for r in range(4):
            total = earlier_sum(r, zh) + up32(rz[r])
            for j in late[r]:
                total += up32(dr[j])
            if r == 2:
                total += OB[NC - 1, :, zh, x]
            total = total.astype(BF)
            source = lax.rem(x + r, 4)
            block_out[:, source] = total[:, :, :WIDTH]
            input_out[:, source] = total[:, :, WIDTH:]

    def pair_grads():
        tn = (((0,), (0,)), ((), ()))
        acts = G[0].reshape(1024, WIDTH)
        for first, to in ((HID, tg), (2 * HID, tu)):
            def unit(u, carry, first=first, to=to):
                cols = pl.ds(pl.multiple_of(u * UNIT + first, 128), UNIT)
                h = H[:, :, :, :, cols].reshape(1024, UNIT)
                part = lax.dot_general(acts, h, tn, preferred_element_type=F32)
                to[:, pl.ds(pl.multiple_of(u * UNIT, 128), UNIT)] = (part * (1.0 / 32.0)).astype(BF)
                return carry
            lax.fori_loop(0, 3, unit, 0)
        local_copy(tg, gate_out)
        local_copy(tu, up_out)

    def down_grads():
        tn = (((0,), (0,)), ((), ()))
        grads = G[1].reshape(1024, WIDTH)

        def unit(u, carry):
            cols = pl.ds(pl.multiple_of(u * UNIT, 128), UNIT)
            h = H[:, :, :, :, cols].reshape(1024, UNIT)
            part = lax.dot_general(h, grads, tn, preferred_element_type=F32)
            td[cols, :] = (part * (1.0 / 32.0)).astype(BF)
            return carry
        lax.fori_loop(0, 3, unit, 0)
        local_copy(td, down_out)

    def seq_one():
        for name in ("xoa+", "xpa+", "xoa-", "xpa-", "xog+", "xpg+", "xog-", "xpg-"):
            recv(name, 0)
        send("xf+", 0, G.at[:, 1, 0], G.at[:, 3, 0], XP)
        send("xf-", 0, G.at[:, 2, 1], G.at[:, 3, 1], XM)
        for k in (1, 2):
            send("qa", k, G.at[0, k, oc], Q.at[0, k], CO)
            send("qg", k, G.at[1, k, oc], Q.at[1, k], CO)

    def seq_two():
        recv("xf+", 0)
        recv("xf-", 0)
        send("qa", 3, G.at[0, 3, oc], Q.at[0, 3], CO)
        send("qg", 3, G.at[1, 3, oc], Q.at[1, 3], CO)

    stages = [forward, reduce_one, reduce_two, finish, gather_one, gather_two, gather_three]
    for slot in range(NC + len(stages)):
        if slot < NC:
            forward(slot)
        if slot == 0:
            seq_one()
        if slot == 2:
            seq_two()
        for k in range(NC):
            stage = slot - k
            if 1 <= stage < len(stages):
                stages[stage](k)
        if 0 <= slot - len(stages) < NC:
            last(slot - len(stages))
    pair_grads()
    seq_exchange()
    down_grads()
    seq_finish()
    for cp in copies.values():
        cp.wait_send()
    for cp in local[len(loads):]:
        cp.wait()


def run_mega(acts, grads, lengths, dest, mask, adv, gate, up, down):
    vm = pltpu.VMEM
    shape = jax.ShapeDtypeStruct
    rows = shape((2, 4, BIN, WIDTH), BF)
    wide, tall = shape((WIDTH, HID), BF), shape((HID, WIDTH), BF)
    hbm = pl.BlockSpec(memory_space=pl.ANY)
    whole = pl.BlockSpec(memory_space=vm)
    return pl.pallas_call(
        mega,
        out_shape=(rows, rows, wide, wide, tall),
        in_specs=[whole] * 6 + [hbm] * 3,
        out_specs=(whole, whole, hbm, hbm, hbm),
        scratch_shapes=[
            vm((WIDTH, HID), BF), vm((WIDTH, HID), BF), vm((HID, WIDTH), BF),
            vm((WIDTH, HID), BF), vm((WIDTH, HID), BF), vm((HID, WIDTH), BF),
            vm((2, NC, 2, 128, WIDTH), BF),
            vm((2, NC, 128, WIDTH), BF),
            vm((NC, 8, BIN, ALL), BF),
            vm((NC, 2, 8, BIN, ALL), BF),
            vm((NC, 2, BIN, CY), BF), vm((NC, 2, BIN, CY), BF), vm((NC, 2, BIN, CY), BF),
            vm((NC, BIN, CY), BF), vm((NC, BIN, CY), BF),
            vm((NC, 4, BIN, CZ), BF),
            vm((NC, 2, BIN, HZ), BF), vm((NC, 2, BIN, HZ), BF), vm((NC, 2, BIN, HZ), BF),
            vm((BIN, ALL), F32),
            vm((NC, 2, 2, 4, BIN, 2 * WIDTH), F32),
            vm((2, 2, 4, BIN, 2 * WIDTH), BF),
            vm((NC - 1, 2, 2, BIN, 2 * WIDTH), F32),
            vm((NC - 1, 2, 2, BIN, 2 * WIDTH), F32),
            vm((NC - 1, 2, 2, BIN, 2 * WIDTH), F32),
            vm((4, 2, BIN, 2 * WIDTH), BF), vm((4, 2, BIN, 2 * WIDTH), BF),
            vm((7, 2, BIN, 2 * WIDTH), BF),
            vm((WIDTH, HID), BF), vm((WIDTH, HID), BF), vm((HID, WIDTH), BF),
            pltpu.SemaphoreType.DMA((N_SEM,)),
            pltpu.SemaphoreType.DMA((N_SEM,)),
            pltpu.SemaphoreType.DMA((8,)),
        ],
        compiler_params=pltpu.CompilerParams(
            collective_id=0, has_side_effects=True, vmem_limit_bytes=62 * 2**20
        ),
        name="mega",
    )(acts, grads, lengths, dest, mask, adv, gate, up, down)


def per_device(
    rollout_acts, rollout_grads, lengths, destination, valid_mask, advantage,
    gate_weight, up_weight, down_weight,
):
    block, inner, gate_grad, up_grad, down_grad = run_mega(
        rollout_acts, rollout_grads, lengths, destination, valid_mask[None, :], advantage,
        gate_weight, up_weight, down_weight,
    )
    return (
        block.reshape(128, WIDTH), inner.reshape(128, WIDTH),
        gate_grad.astype(F32), up_grad.astype(F32), down_grad.astype(F32),
    )


def solution(mesh):
    return jax.shard_map(
        per_device,
        mesh=mesh,
        in_specs=(
            P("seq", "tp"), P("seq", "tp"), P("seq", None), P("seq", None), P("seq"),
            P("seq", None), P("tp", "seq"), P("tp", "seq"), P("seq", "tp"),
        ),
        out_specs=(P("seq", "tp"), P("seq", "tp"), P("tp", "seq"), P("tp", "seq"), P("seq", "tp")),
        check_vma=False,
    )
```

```python
import jax
import jax.numpy as jnp
from jax import lax
from jax.experimental import pallas as pl
from jax.experimental.pallas import tpu as pltpu
from jax.sharding import PartitionSpec as P

BIN = 16
NS = 4
WIDTH = 512
HID = 1920
PARTS = (1920,)
YCOLS = (3456,)
NP = len(PARTS)
NK = NS * NP
BASES = tuple(sum(PARTS[:j]) for j in range(NP))
ALL = 3 * HID
MAXY = max(YCOLS)
MAXZ = max(3 * h - w for h, w in zip(PARTS, YCOLS))
BF = jnp.bfloat16
F32 = jnp.float32
MESH = pl.DeviceIdType.MESH
NT = (((1,), (1,)), ((), ()))
TN = (((0,), (0,)), ((), ()))

ORDER = (
    ("pro", 0), ("pro2", 0), ("wl", 0), ("zha", 0), ("zhg", 0), ("fa", 0), ("fb", 0), ("sx", 0), ("ya+", 0),
    ("ya-", 0), ("fa", 1), ("fb", 1), ("yz", 0), ("sy", 0), ("zr", 0), ("fa", 2), ("ya+", 1), ("ya-", 1),
    ("fb", 2), ("ra+", 0), ("ra-", 0), ("zr", 1), ("ya+", 2), ("ya-", 2), ("yz", 1), ("fin", 0), ("ra+", 1),
    ("ra-", 1), ("zr", 2), ("yz", 2), ("ap", 0), ("af+", 0), ("bp", 0), ("bm", 0), ("ca", 0), ("fin", 1),
    ("ra+", 2), ("ra-", 2), ("af-", 0), ("ap", 1), ("b3", 0), ("fa", 3), ("bm", 1), ("af+", 1), ("fb", 3),
    ("bp", 1), ("ca", 1), ("fin", 2), ("cc", 0), ("af-", 1), ("last", 0), ("ya+", 3), ("ya-", 3), ("zr", 3),
    ("b3", 1), ("ap", 2), ("bm", 2), ("af+", 2), ("bp", 2), ("cc", 1), ("ca", 2), ("yz", 3), ("ra+", 3),
    ("ra-", 3), ("last", 1), ("af-", 2), ("b3", 2), ("fin", 3), ("cc", 2), ("af+", 3), ("ap", 3),
    ("last", 2), ("bp", 3), ("bm", 3), ("ca", 3), ("af-", 3), ("b3", 3), ("sz", 0), ("cc", 3), ("last", 3),
    ("wgrad", 0), ("end", 0),
)

SEQ_NAMES = (
    "zha", "zhg", "xoa+", "xoa-", "xog+", "xog-", "xpa+", "xpa-", "xpg+", "xpg-", "xf+", "xf-",
    "sz", "dx+", "dx-", "dx2", "dz", "dzx+", "dzx-", "dzx2",
)
PIECE_NAMES = (
    "y1+", "y1-", "yo+", "yo-", "ya+", "ya-", "yz",
    "z1", "r1+", "r1-", "ro+", "ro-", "ra+", "ra-",
    "az", "ay+", "ay-", "by+", "by-", "bz0", "ap+", "ap-", "bf+", "bf-",
    "bz1", "bz2", "af+", "af-", "bz3", "ca0", "ca1", "ca2", "cc0", "cc1",
)
SEM = {}
for _n in SEQ_NAMES:
    SEM[(_n, 0)] = len(SEM)
for _k in range(NP):
    for _n in ("wg", "wu", "wd"):
        SEM[(_n, _k)] = len(SEM)
for _k in range(NS):
    for _n in ("qa", "qg", "m+", "m-", "m2"):
        SEM[(_n, _k)] = len(SEM)
for _k in range(NK):
    for _n in PIECE_NAMES:
        SEM[(_n, _k)] = len(SEM)
N_SEM = len(SEM)


def up32(value):
    return value.astype(F32)


def routing(lengths, destination, advantage, mask):
    diagonal = lax.broadcasted_iota(jnp.int32, (16, 16), 0) == lax.broadcasted_iota(jnp.int32, (16, 16), 1)

    def column(row):
        return jnp.sum(jnp.where(diagonal, row, jnp.zeros_like(row)), axis=1, keepdims=True)

    resp = lax.broadcasted_iota(jnp.int32, (16, 256), 0)
    row = lax.broadcasted_iota(jnp.int32, (16, 256), 1)
    of_row = row // BIN
    mine = of_row == resp

    def spread(col):
        return jnp.sum(jnp.where(mine, col, jnp.zeros_like(col)), axis=0, keepdims=True)

    len_col, dest_col = column(lengths), column(destination)
    len_row, dest_row = spread(len_col), spread(dest_col)
    before = (dest_col == dest_row) & (resp < of_row)
    offset = jnp.sum(jnp.where(before, len_col, 0), axis=0, keepdims=True)
    within = lax.rem(row[:1], BIN)
    slot = jnp.where(within < len_row, dest_row * BIN + offset + within, -1)
    hot = lax.broadcasted_iota(jnp.int32, (128, 256), 0) == slot
    weight = spread(column(advantage)) * mask.astype(F32)
    weight = jnp.sum(jnp.where(hot, weight, 0.0), axis=1, keepdims=True)
    return jnp.where(hot, 1.0, 0.0).astype(BF), weight


def mega(
    acts_ref, grads_ref, lengths_ref, dest_ref, mask_ref, adv_ref, gate_hbm, up_hbm, down_hbm,
    block_out, input_out, gate_out, up_out, down_out,
    wg, wu, wd, pg, pu, pd, G, Q, RY, RZ, FY, FZ, H,
    y1, yown, yacc, ysend, yz, z1, r1, rown, racc, F,
    OB, OL, rm, rp, r2, sz, rz, dr, tg, tu, td,
    ssem, rsem, lsem,
):
    s = lax.axis_index("seq")
    t = lax.axis_index("tp")
    zh, x = s // 4, lax.rem(s, 4)
    zl, y, c = t // 8, lax.rem(t // 2, 4), lax.rem(t, 2)
    oz, oc, oh = 1 - zl, 1 - c, 1 - zh
    yp, ym, y2 = lax.rem(y + 1, 4), lax.rem(y + 3, 4), lax.rem(y + 2, 4)
    xp, xm, x2 = lax.rem(x + 1, 4), lax.rem(x + 3, 4), lax.rem(x + 2, 4)

    def dev(zh_=zh, x_=x, zl_=zl, y_=y, c_=c):
        return (zh_ * 4 + x_, zl_ * 8 + y_ * 2 + c_)

    XP, XM, X2 = dev(x_=xp), dev(x_=xm), dev(x_=x2)
    YP, YM = dev(y_=yp), dev(y_=ym)
    ZL, ZH, CO = dev(zl_=oz), dev(zh_=oh), dev(c_=oc)

    copies = {}

    def send(name, k, src, dst, to):
        i = SEM[(name, k)]
        cp = pltpu.make_async_remote_copy(
            src_ref=src, dst_ref=dst, send_sem=ssem.at[i], recv_sem=rsem.at[i],
            device_id=to, device_id_type=MESH,
        )
        cp.start()
        copies[(name, k)] = cp

    def recv(k, *names):
        for name in names:
            copies[(name, k)].wait_recv()

    local = []

    def local_copy(src, dst):
        cp = pltpu.make_async_copy(src, dst, lsem.at[len(local)])
        cp.start()
        local.append(cp)
        return cp

    def src_of(k):
        return k // NP

    def hid_of(k):
        return pl.ds(BASES[k % NP], PARTS[k % NP])

    def sizes(k):
        h, w = PARTS[k % NP], YCOLS[k % NP]
        return h, w, 3 * h - w, (3 * h - w) // 2

    def all_cols(k):
        return pl.ds(3 * BASES[k % NP], 3 * PARTS[k % NP])

    def y_cols(k):
        return pl.ds(3 * BASES[k % NP], YCOLS[k % NP])

    def z_cols(k):
        return pl.ds(3 * BASES[k % NP] + YCOLS[k % NP], sizes(k)[2])

    def z_half(k, half):
        return pl.ds(3 * BASES[k % NP] + YCOLS[k % NP] + half * sizes(k)[3], sizes(k)[3])

    loads = [local_copy(gate_hbm, wg), local_copy(up_hbm, wu), local_copy(down_hbm, wd)]
    barrier = pltpu.get_barrier_semaphore()
    peers = [XP, XM, YP, YM, ZL, ZH, CO, X2]
    peers += [dev(zh_=oh, x_=x_) for x_ in (xp, xm, x2)]
    for peer in peers:
        pl.semaphore_signal(barrier, inc=1, device_id=peer, device_id_type=MESH)
    hot, weight = routing(lengths_ref[...], dest_ref[...], adv_ref[...], mask_ref[...])

    def spread_own(arr, n):
        send("zh" + n, 0, G.at[arr, 0, zh], G.at[arr, 0, zh], ZH)
        send("xo" + n + "+", 0, G.at[arr, 0, zh], G.at[arr, 1, zh], XP)
        send("xo" + n + "-", 0, G.at[arr, 0, zh], G.at[arr, 2, zh], XM)

    def spread_peer(arr, n):
        recv(0, "zh" + n)
        send("q" + n, 0, G.at[arr, 0, oc], Q.at[arr, 0], CO)
        send("xp" + n + "+", 0, G.at[arr, 0, oh], G.at[arr, 1, oh], XP)
        send("xp" + n + "-", 0, G.at[arr, 0, oh], G.at[arr, 2, oh], XM)

    def pack_acts(k):
        G[0, 0, zh] = jnp.dot(hot, acts_ref[...], preferred_element_type=F32).astype(BF)
        pl.semaphore_wait(barrier, len(peers))
        spread_own(0, "a")

    def pack_grads(k):
        packed = jnp.dot(hot, grads_ref[...], preferred_element_type=F32)
        G[1, 0, zh] = (packed * weight).astype(BF)
        spread_own(1, "g")

    def swap_weights(k):
        for cp in loads:
            cp.wait()
        for j in range(NP):
            hid = hid_of(j)
            send("wg", j, wg.at[:, hid], pg.at[:, hid], CO)
            send("wu", j, wu.at[:, hid], pu.at[:, hid], CO)
            send("wd", j, wd.at[hid], pd.at[hid], CO)

    def peer_acts(k):
        spread_peer(0, "a")

    def peer_grads(k):
        spread_peer(1, "g")

    def pass_on(k):
        recv(0, "xoa+", "xpa+", "xoa-", "xpa-", "xog+", "xpg+", "xog-", "xpg-")
        send("xf+", 0, G.at[:, 1, 0], G.at[:, 3, 0], XP)
        send("xf-", 0, G.at[:, 2, 1], G.at[:, 3, 1], XM)
        for n in (1, 2):
            send("qa", n, G.at[0, n, oc], Q.at[0, n], CO)
            send("qg", n, G.at[1, n, oc], Q.at[1, n], CO)

    def far_rows(k):
        recv(0, "xf+", "xf-")
        send("qa", 3, G.at[0, 3, oc], Q.at[0, 3], CO)
        send("qg", 3, G.at[1, 3, oc], Q.at[1, 3], CO)

    Y_ORDER = ((0, y2), (1, y2), (1, yp), (0, ym), (0, yp), (1, ym), (0, y), (1, y))
    Z_ORDER = tuple((oz, n) for n in range(4)) + tuple((zl, n) for n in range(4))

    def rows_in(ref, index, order):
        return jnp.concatenate(
            [ref[index + (pl.ds(pl.multiple_of((a * 4 + b) * BIN, BIN), BIN),)] for a, b in order], axis=0
        )

    def keep(raw, full, k, first, part):
        width = part.shape[1]
        raw[k, :, :, first:first + width] = part[:64].astype(BF).reshape(4, BIN, width)
        full[k, :, :, first:first + width] = part[64:].reshape(4, BIN, width)

    def product(a, b, own, par):
        return jnp.dot(a, own, preferred_element_type=F32) + jnp.dot(b, par, preferred_element_type=F32)

    def forward_y(k):
        n, j = src_of(k), k % NP
        h, w, _, _ = sizes(k)
        base = BASES[j]
        recv(n, "qa") if j == 0 else None
        recv(j, "wg", "wu") if n == 0 else None
        a, b = rows_in(G, (0, n, c), Y_ORDER), rows_in(Q, (0, n), Y_ORDER)
        cols = slice(base, base + h)
        keep(RY, FY, k, 0, product(a, b, wg[:, cols], pg[:, cols]))
        cols = slice(base, base + w - h)
        keep(RY, FY, k, h, product(a, b, wu[:, cols], pu[:, cols]))
        send("y1+", k, RY.at[k, 0, :, pl.ds(0, w)], y1.at[k, 0, :, pl.ds(0, w)], YP)
        send("y1-", k, RY.at[k, 1, :, pl.ds(0, w)], y1.at[k, 1, :, pl.ds(0, w)], YM)
        send("yo+", k, RY.at[k, 2, :, pl.ds(0, w)], yown.at[k, 1, :, pl.ds(0, w)], YP)
        send("yo-", k, RY.at[k, 3, :, pl.ds(0, w)], yown.at[k, 0, :, pl.ds(0, w)], YM)

    def forward_z(k):
        n, j = src_of(k), k % NP
        h, w, v, _ = sizes(k)
        base = BASES[j]
        a, b = rows_in(G, (0, n, c), Z_ORDER), rows_in(Q, (0, n), Z_ORDER)
        cols = slice(base + w - h, base + h)
        keep(RZ, FZ, k, 0, product(a, b, wu[:, cols], pu[:, cols]))
        recv(n, "qg") if j == 0 else None
        recv(j, "wd") if n == 0 else None
        a, b = rows_in(G, (1, n, c), Z_ORDER), rows_in(Q, (1, n), Z_ORDER)
        part = lax.dot_general(a, wd[base:base + h, :], NT, preferred_element_type=F32)
        part += lax.dot_general(b, pd[base:base + h, :], NT, preferred_element_type=F32)
        keep(RZ, FZ, k, 2 * h - w, part)
        send("z1", k, RZ.at[k, :, :, pl.ds(0, v)], z1.at[k, :, :, pl.ds(0, v)], ZL)

    def pass_y(k, half, name, to):
        w = sizes(k)[1]
        recv(k, "y1" + name)
        y1[k, half, :, :w] = (up32(y1[k, half, :, :w]) + FY[k, half, :, :w]).astype(BF)
        send("ya" + name, k, y1.at[k, half, :, pl.ds(0, w)], yacc.at[k, half, :, pl.ds(0, w)], to)

    def pass_z(k):
        _, _, v, u = sizes(k)
        recv(k, "z1")
        for row in (y2, yp, ym):
            z1[k, row, :, :v] = (up32(z1[k, row, :, :v]) + FZ[k, row, :, :v]).astype(BF)
        low, high = pl.ds(0, u), pl.ds(u, u)
        send("r1+", k, z1.at[k, y2, :, low], r1.at[k, 0, :, low], YP)
        send("r1-", k, z1.at[k, y2, :, high], r1.at[k, 1, :, low], YM)
        send("ro+", k, z1.at[k, yp, :, high], rown.at[k, 1, :, low], YP)
        send("ro-", k, z1.at[k, ym, :, low], rown.at[k, 0, :, low], YM)

    def cross_z(k):
        w = sizes(k)[1]
        recv(k, "yo+", "yo-", "ya+", "ya-")
        total = FY[k, 2 + oz, :, :w] + up32(yacc[k, oz, :, :w]) + up32(yown[k, oz, :, :w])
        ysend[k, :, :w] = total.astype(BF)
        send("yz", k, ysend.at[k, :, pl.ds(0, w)], yz.at[k, :, pl.ds(0, w)], ZL)

    def pass_r(k, half, name, row, to):
        u = sizes(k)[3]
        recv(k, "r1" + name)
        total = up32(r1[k, half, :, :u]) + up32(z1[k, row, :, half * u:half * u + u])
        r1[k, half, :, :u] = total.astype(BF)
        send("ra" + name, k, r1.at[k, half, :, pl.ds(0, u)], racc.at[k, half, :, pl.ds(0, u)], to)

    def finish(k):
        n = src_of(k)
        h, w, v, u = sizes(k)
        base = 3 * BASES[k % NP]
        recv(k, "yz", "ro+", "ro-", "ra+", "ra-")
        mine = zl * 4 + y
        F[:, :w] = (
            FY[k, 2 + zl, :, :w] + up32(yacc[k, zl, :, :w]) + up32(yown[k, zl, :, :w]) + up32(yz[k, :, :w])
        )
        for half in (0, 1):
            cols = slice(half * u, half * u + u)
            F[:, w + half * u:w + half * u + u] = (
                FZ[k, y, :, cols] + up32(z1[k, y, :, cols])
                + up32(racc[k, half, :, :u]) + up32(rown[k, half, :, :u])
            )
        gate, upper, back = F[:, :h], F[:, h:2 * h], F[:, 2 * h:3 * h]
        sigma = jax.nn.sigmoid(gate)
        swish = gate * sigma
        H[n, c, mine, :, base:base + h] = (swish * upper).astype(BF)
        H[n, c, mine, :, base + h:base + 2 * h] = (
            back * upper * sigma * (1.0 + gate * (1.0 - sigma))
        ).astype(BF)
        H[n, c, mine, :, base + 2 * h:base + 3 * h] = (back * swish).astype(BF)
        a = H.at[n, c, mine, :, y_cols(k)]
        b = H.at[n, c, mine, :, z_cols(k)]
        send("az", k, a, a, ZL)
        send("ay+", k, a, a, YP)
        send("ay-", k, a, a, YM)
        send("by+", k, b, b, YP)
        send("by-", k, b, b, YM)
        send("bz0", k, b, b, ZL)

    def move(name, k, plane, row, cols, to):
        part = H.at[src_of(k), c, plane * 4 + row, :, cols]
        send(name, k, part, part, to)

    def plus_b(k):
        recv(k, "by+")
        move("bf+", k, zl, ym, z_half(k, 0), YP)
        move("bz1", k, zl, ym, z_cols(k), ZL)

    def minus_b(k):
        recv(k, "by-")
        move("bf-", k, zl, yp, z_half(k, 1), YM)
        move("bz2", k, zl, yp, z_cols(k), ZL)

    def plane_a(k):
        recv(k, "az")
        move("ap+", k, oz, y, y_cols(k), YP)
        move("ap-", k, oz, y, y_cols(k), YM)

    def plus_a(k):
        recv(k, "ay+")
        move("af+", k, zl, ym, y_cols(k), YP)

    def far_b(k):
        recv(k, "bf+", "bf-")
        move("bz3", k, zl, y2, z_cols(k), ZL)

    def far_a(k):
        recv(k, "ap-")
        move("af-", k, oz, yp, y_cols(k), YM)

    def core_near(k):
        recv(k, "ay-")
        for n, row in enumerate((y, ym, yp)):
            move(f"ca{n}", k, zl, row, all_cols(k), CO)

    def core_far(k):
        recv(k, "af+", "af-", "ap+", "bz0", "bz1", "bz2", "bz3")
        part = H.at[src_of(k), c, pl.ds(oz * 4, 4), :, all_cols(k)]
        send("cc0", k, part, part, CO)
        move("cc1", k, zl, y2, all_cols(k), CO)

    def outputs(k):
        n, j = src_of(k), k % NP
        h = sizes(k)[0]
        base = 3 * BASES[j]
        hid = slice(BASES[j], BASES[j] + h)
        recv(k, "ca0", "ca1", "ca2", "cc0", "cc1")
        shape = (2, 2, 4, BIN, WIDTH)
        first = H[n, :, :, :, base:base + h].reshape(256, h)
        block = jnp.dot(first, wd[hid, :], preferred_element_type=F32).reshape(shape)
        first = H[n, :, :, :, base + h:base + 2 * h].reshape(256, h)
        inner = lax.dot_general(first, wg[:, hid], NT, preferred_element_type=F32)
        first = H[n, :, :, :, base + 2 * h:base + 3 * h].reshape(256, h)
        inner += lax.dot_general(first, wu[:, hid], NT, preferred_element_type=F32)
        inner = inner.reshape(shape)
        if j > 0:
            block += OB[n, :, :, :, :, :WIDTH]
            inner += OB[n, :, :, :, :, WIDTH:]
        OB[n, :, :, :, :, :WIDTH] = block
        OB[n, :, :, :, :, WIDTH:] = inner
        if j < NP - 1:
            return
        OL[n, :, :, :, :, :WIDTH] = block.astype(BF)
        OL[n, :, :, :, :, WIDTH:] = inner.astype(BF)
        if n < NS - 1:
            send("m+", n, OL.at[n, :, :, xp], rm.at[n], XP)
            send("m-", n, OL.at[n, :, :, xm], rp.at[n], XM)
            send("m2", n, OL.at[n, :, :, x2], r2.at[n], X2)
        else:
            send("dzx2", 0, OL.at[n, :, oh, x2], dr.at[6], dev(zh_=oh, x_=x2))
            send("dzx+", 0, OL.at[n, :, oh, xp], dr.at[4], dev(zh_=oh, x_=xp))
            send("dzx-", 0, OL.at[n, :, oh, xm], dr.at[5], dev(zh_=oh, x_=xm))
            send("dz", 0, OL.at[n, :, oh, x], dr.at[3], ZH)
            send("dx2", 0, OL.at[n, :, zh, x2], dr.at[2], X2)
            send("dx+", 0, OL.at[n, :, zh, xp], dr.at[0], XP)
            send("dx-", 0, OL.at[n, :, zh, xm], dr.at[1], XM)

    PLACES = ((0, 2, 1, 3), (2, 3, 0, 1), (3, 1, 2, 0), (1, 0, 3, 2))

    def earlier_sum(r, half):
        total = None
        for n, ref in zip(PLACES[r], (None, rm, rp, r2)):
            if n < NS - 1:
                part = OB[n, :, half, x] if ref is None else up32(ref[n, :, half])
                total = part if total is None else total + part
        return total

    def seq_exchange(k):
        for n in range(NS - 1):
            recv(n, "m+", "m-", "m2")
        for r in range(4):
            sz[r] = earlier_sum(r, oh).astype(BF)
        send("sz", 0, sz, rz, ZH)

    def seq_finish(k):
        recv(0, "dx+", "dx-", "dx2", "dz", "dzx+", "dzx-", "dzx2", "sz")
        late = {0: (2, 6), 1: (0, 4), 2: (3,), 3: (1, 5)}
        for r in range(4):
            total = earlier_sum(r, zh) + up32(rz[r])
            for j in late[r]:
                total += up32(dr[j])
            if r == 2:
                total += OB[NS - 1, :, zh, x]
            total = total.astype(BF)
            source = lax.rem(x + r, 4)
            block_out[:, source] = total[:, :, :WIDTH]
            input_out[:, source] = total[:, :, WIDTH:]

    def weight_grads(k):
        acts = G[0].reshape(1024, WIDTH)
        grads = G[1].reshape(1024, WIDTH)
        for j in range(NP):
            h = PARTS[j]
            for at in range(0, h, 512):
                width = min(512, h - at)
                to = pl.ds(BASES[j] + at, width)
                for place, out in ((1, tg), (2, tu)):
                    cols = pl.ds(3 * BASES[j] + place * h + at, width)
                    part = H[:, :, :, :, cols].reshape(1024, width)
                    part = lax.dot_general(acts, part, TN, preferred_element_type=F32)
                    out[:, to] = (part * (1.0 / 32.0)).astype(BF)
                part = H[:, :, :, :, pl.ds(3 * BASES[j] + at, width)].reshape(1024, width)
                part = lax.dot_general(part, grads, TN, preferred_element_type=F32)
                td[to, :] = (part * (1.0 / 32.0)).astype(BF)
        local_copy(tg, gate_out)
        local_copy(tu, up_out)
        local_copy(td, down_out)

    steps = {
        "pro": pack_acts, "pro2": pack_grads, "wl": swap_weights, "zha": peer_acts, "zhg": peer_grads,
        "sx": pass_on, "sy": far_rows, "fa": forward_y, "fb": forward_z,
        "ya+": lambda k: pass_y(k, 0, "+", YP), "ya-": lambda k: pass_y(k, 1, "-", YM),
        "zr": pass_z, "yz": cross_z,
        "ra+": lambda k: pass_r(k, 0, "+", yp, YP), "ra-": lambda k: pass_r(k, 1, "-", ym, YM),
        "fin": finish, "bp": plus_b, "bm": minus_b, "ap": plane_a, "af+": plus_a,
        "b3": far_b, "af-": far_a, "ca": core_near, "cc": core_far, "last": outputs,
        "sz": seq_exchange, "wgrad": weight_grads, "end": seq_finish,
    }
    for name, k in ORDER:
        steps[name](k)
    for cp in copies.values():
        cp.wait_send()
    for cp in local[len(loads):]:
        cp.wait()


def run_mega(acts, grads, lengths, dest, mask, adv, gate, up, down):
    vm = pltpu.VMEM
    shape = jax.ShapeDtypeStruct
    rows = shape((2, 4, BIN, WIDTH), BF)
    wide, tall = shape((WIDTH, HID), BF), shape((HID, WIDTH), BF)
    hbm = pl.BlockSpec(memory_space=pl.ANY)
    whole = pl.BlockSpec(memory_space=vm)
    late = vm((NS - 1, 2, 2, BIN, 2 * WIDTH), BF)
    ybuf, zbuf = vm((NK, 2, BIN, MAXY), BF), vm((NK, 2, BIN, MAXZ // 2), BF)
    return pl.pallas_call(
        mega,
        out_shape=(rows, rows, wide, wide, tall),
        in_specs=[whole] * 6 + [hbm] * 3,
        out_specs=(whole, whole, hbm, hbm, hbm),
        scratch_shapes=[
            vm((WIDTH, HID), BF), vm((WIDTH, HID), BF), vm((HID, WIDTH), BF),
            vm((WIDTH, HID), BF), vm((WIDTH, HID), BF), vm((HID, WIDTH), BF),
            vm((2, NS, 2, 128, WIDTH), BF),
            vm((2, NS, 128, WIDTH), BF),
            vm((NK, 4, BIN, MAXY), BF), vm((NK, 4, BIN, MAXZ), BF),
            vm((NK, 4, BIN, MAXY), F32), vm((NK, 4, BIN, MAXZ), F32),
            vm((NS, 2, 8, BIN, ALL), BF),
            ybuf, ybuf, ybuf,
            vm((NK, BIN, MAXY), BF), vm((NK, BIN, MAXY), BF),
            vm((NK, 4, BIN, MAXZ), BF),
            zbuf, zbuf, zbuf,
            vm((BIN, 3 * max(PARTS)), F32),
            vm((NS, 2, 2, 4, BIN, 2 * WIDTH), F32),
            vm((NS, 2, 2, 4, BIN, 2 * WIDTH), BF),
            late, late, late,
            vm((4, 2, BIN, 2 * WIDTH), BF), vm((4, 2, BIN, 2 * WIDTH), BF),
            vm((7, 2, BIN, 2 * WIDTH), BF),
            vm((WIDTH, HID), BF), vm((WIDTH, HID), BF), vm((HID, WIDTH), BF),
            pltpu.SemaphoreType.DMA((N_SEM,)),
            pltpu.SemaphoreType.DMA((N_SEM,)),
            pltpu.SemaphoreType.DMA((8,)),
        ],
        compiler_params=pltpu.CompilerParams(
            collective_id=0, has_side_effects=True, vmem_limit_bytes=62 * 2**20
        ),
        name="mega",
    )(acts, grads, lengths, dest, mask, adv, gate, up, down)


def per_device(
    rollout_acts, rollout_grads, lengths, destination, valid_mask, advantage,
    gate_weight, up_weight, down_weight,
):
    block, inner, gate_grad, up_grad, down_grad = run_mega(
        rollout_acts, rollout_grads, lengths, destination, valid_mask[None, :], advantage,
        gate_weight, up_weight, down_weight,
    )
    return (
        block.reshape(128, WIDTH), inner.reshape(128, WIDTH),
        gate_grad.astype(F32), up_grad.astype(F32), down_grad.astype(F32),
    )


def solution(mesh):
    return jax.shard_map(
        per_device,
        mesh=mesh,
        in_specs=(
            P("seq", "tp"), P("seq", "tp"), P("seq", None), P("seq", None), P("seq"),
            P("seq", None), P("tp", "seq"), P("tp", "seq"), P("seq", "tp"),
        ),
        out_specs=(P("seq", "tp"), P("seq", "tp"), P("tp", "seq"), P("tp", "seq"), P("seq", "tp")),
        check_vma=False,
    )
```

```python
import jax
import jax.numpy as jnp
from jax import lax
from jax.experimental import pallas as pl
from jax.experimental.pallas import tpu as pltpu
from jax.sharding import PartitionSpec as P

BIN = 16
NS = 4
WIDTH = 512
HID = 1920
PARTS = (1024, 896)
YCOLS = (1792, 1664)
NP = len(PARTS)
NK = NS * NP
BASES = tuple(sum(PARTS[:j]) for j in range(NP))
ALL = 3 * HID
MAXY = max(YCOLS)
MAXZ = max(3 * h - w for h, w in zip(PARTS, YCOLS))
BF = jnp.bfloat16
F32 = jnp.float32
MESH = pl.DeviceIdType.MESH
NT = (((1,), (1,)), ((), ()))
TN = (((0,), (0,)), ((), ()))

ORDER = (
    0, 10, 20, 30, 40, 70, 80, 71, 50, 81, 90, 100, 72, 82, 91, 101, 110, 120, 111, 92, 102, 60, 73, 83,
    130, 140, 121, 131, 141, 112, 74, 122, 84, 93, 103, 113, 150, 151, 132, 142, 94, 104, 123, 133, 143,
    114, 180, 190, 160, 170, 220, 181, 191, 161, 171, 221, 152, 124, 153, 134, 144, 210, 182, 200, 211, 75,
    85, 172, 201, 183, 192, 173, 162, 222, 193, 230, 163, 223, 154, 212, 115, 231, 240, 95, 105, 241, 213,
    184, 202, 174, 203, 194, 232, 145, 164, 224, 135, 76, 125, 233, 86, 214, 77, 87, 204, 242, 155, 96, 106,
    243, 116, 97, 107, 195, 117, 165, 234, 175, 225, 126, 136, 185, 146, 244, 127, 137, 147, 205, 215, 156,
    157, 235, 186, 196, 166, 176, 226, 245, 187, 197, 167, 177, 227, 216, 206, 217, 207, 236, 250, 246, 237,
    247, 260, 270,
)

SEQ_NAMES = (
    "zha", "zhg", "xoa+", "xoa-", "xog+", "xog-", "xpa+", "xpa-", "xpg+", "xpg-", "xf+", "xf-",
    "sz", "dx+", "dx-", "dx2", "dz", "dzx+", "dzx-", "dzx2",
)
PIECE_NAMES = (
    "y1+", "y1-", "yo+", "yo-", "ya+", "ya-", "yz",
    "z1", "r1+", "r1-", "ro+", "ro-", "ra+", "ra-",
    "az", "ay+", "ay-", "by+", "by-", "bz0", "ap+", "ap-", "bf+", "bf-",
    "bz1", "bz2", "af+", "af-", "bz3", "ca0", "ca1", "ca2", "cc0", "cc1",
)
SEM = {}
for _n in SEQ_NAMES:
    SEM[(_n, 0)] = len(SEM)
for _k in range(NP):
    for _n in ("wg", "wu", "wd"):
        SEM[(_n, _k)] = len(SEM)
for _k in range(NS):
    for _n in ("qa", "qg", "m+", "m-", "m2"):
        SEM[(_n, _k)] = len(SEM)
for _k in range(NK):
    for _n in PIECE_NAMES:
        SEM[(_n, _k)] = len(SEM)
N_SEM = len(SEM)


def up32(value):
    return value.astype(F32)


def routing(lengths, destination, advantage, mask):
    diagonal = lax.broadcasted_iota(jnp.int32, (16, 16), 0) == lax.broadcasted_iota(jnp.int32, (16, 16), 1)

    def column(row):
        return jnp.sum(jnp.where(diagonal, row, jnp.zeros_like(row)), axis=1, keepdims=True)

    resp = lax.broadcasted_iota(jnp.int32, (16, 256), 0)
    row = lax.broadcasted_iota(jnp.int32, (16, 256), 1)
    of_row = row // BIN
    mine = of_row == resp

    def spread(col):
        return jnp.sum(jnp.where(mine, col, jnp.zeros_like(col)), axis=0, keepdims=True)

    len_col, dest_col = column(lengths), column(destination)
    len_row, dest_row = spread(len_col), spread(dest_col)
    before = (dest_col == dest_row) & (resp < of_row)
    offset = jnp.sum(jnp.where(before, len_col, 0), axis=0, keepdims=True)
    within = lax.rem(row[:1], BIN)
    slot = jnp.where(within < len_row, dest_row * BIN + offset + within, -1)
    hot = lax.broadcasted_iota(jnp.int32, (128, 256), 0) == slot
    weight = spread(column(advantage)) * mask.astype(F32)
    weight = jnp.sum(jnp.where(hot, weight, 0.0), axis=1, keepdims=True)
    return jnp.where(hot, 1.0, 0.0).astype(BF), weight


def mega(
    acts_ref, grads_ref, lengths_ref, dest_ref, mask_ref, adv_ref, gate_hbm, up_hbm, down_hbm,
    block_out, input_out, tg, tu, td,
    wg, wu, wd, pg, pu, pd, G, Q, RY, RZ, FY, FZ, H,
    y1, yown, yacc, ysend, yz, z1, r1, rown, racc, F,
    OB, OL, rm, rp, r2, sz, rz, dr,
    ssem, rsem, lsem,
):
    s = lax.axis_index("seq")
    t = lax.axis_index("tp")
    zh, x = s // 4, lax.rem(s, 4)
    zl, y, c = t // 8, lax.rem(t // 2, 4), lax.rem(t, 2)
    oz, oc, oh = 1 - zl, 1 - c, 1 - zh
    yp, ym, y2 = lax.rem(y + 1, 4), lax.rem(y + 3, 4), lax.rem(y + 2, 4)
    xp, xm, x2 = lax.rem(x + 1, 4), lax.rem(x + 3, 4), lax.rem(x + 2, 4)

    def dev(zh_=zh, x_=x, zl_=zl, y_=y, c_=c):
        return (zh_ * 4 + x_, zl_ * 8 + y_ * 2 + c_)

    XP, XM, X2 = dev(x_=xp), dev(x_=xm), dev(x_=x2)
    YP, YM = dev(y_=yp), dev(y_=ym)
    ZL, ZH, CO = dev(zl_=oz), dev(zh_=oh), dev(c_=oc)

    copies = {}

    def send(name, k, src, dst, to):
        i = SEM[(name, k)]
        cp = pltpu.make_async_remote_copy(
            src_ref=src, dst_ref=dst, send_sem=ssem.at[i], recv_sem=rsem.at[i],
            device_id=to, device_id_type=MESH,
        )
        cp.start()
        copies[(name, k)] = cp

    def recv(k, *names):
        for name in names:
            copies[(name, k)].wait_recv()

    local = []

    def local_copy(src, dst):
        cp = pltpu.make_async_copy(src, dst, lsem.at[len(local)])
        cp.start()
        local.append(cp)
        return cp

    def src_of(k):
        return k // NP

    def hid_of(k):
        return pl.ds(BASES[k % NP], PARTS[k % NP])

    def sizes(k):
        h, w = PARTS[k % NP], YCOLS[k % NP]
        return h, w, 3 * h - w, (3 * h - w) // 2

    def all_cols(k):
        return pl.ds(3 * BASES[k % NP], 3 * PARTS[k % NP])

    def y_cols(k):
        return pl.ds(3 * BASES[k % NP], YCOLS[k % NP])

    def z_cols(k):
        return pl.ds(3 * BASES[k % NP] + YCOLS[k % NP], sizes(k)[2])

    def z_half(k, half):
        return pl.ds(3 * BASES[k % NP] + YCOLS[k % NP] + half * sizes(k)[3], sizes(k)[3])

    loads = [local_copy(gate_hbm, wg), local_copy(up_hbm, wu), local_copy(down_hbm, wd)]
    barrier = pltpu.get_barrier_semaphore()
    peers = [XP, XM, YP, YM, ZL, ZH, CO, X2]
    for peer in peers:
        pl.semaphore_signal(barrier, inc=1, device_id=peer, device_id_type=MESH)
    hot, weight = routing(lengths_ref[...], dest_ref[...], adv_ref[...], mask_ref[...])

    def spread_own(arr, n):
        send("zh" + n, 0, G.at[arr, 0, zh], G.at[arr, 0, zh], ZH)
        send("xo" + n + "+", 0, G.at[arr, 0, zh], G.at[arr, 1, zh], XP)
        send("xo" + n + "-", 0, G.at[arr, 0, zh], G.at[arr, 2, zh], XM)

    def spread_peer(arr, n):
        recv(0, "zh" + n)
        send("q" + n, 0, G.at[arr, 0, oc], Q.at[arr, 0], CO)
        send("xp" + n + "+", 0, G.at[arr, 0, oh], G.at[arr, 1, oh], XP)
        send("xp" + n + "-", 0, G.at[arr, 0, oh], G.at[arr, 2, oh], XM)

    def pack_acts(k):
        G[0, 0, zh] = jnp.dot(hot, acts_ref[...], preferred_element_type=F32).astype(BF)
        pl.semaphore_wait(barrier, len(peers))
        spread_own(0, "a")

    def pack_grads(k):
        packed = jnp.dot(hot, grads_ref[...], preferred_element_type=F32)
        G[1, 0, zh] = (packed * weight).astype(BF)
        spread_own(1, "g")

    def swap_weights(k):
        for cp in loads:
            cp.wait()
        for j in range(NP):
            hid = hid_of(j)
            send("wg", j, wg.at[:, hid], pg.at[:, hid], CO)
            send("wu", j, wu.at[:, hid], pu.at[:, hid], CO)
            send("wd", j, wd.at[hid], pd.at[hid], CO)

    def peer_acts(k):
        spread_peer(0, "a")

    def peer_grads(k):
        spread_peer(1, "g")

    def pass_on(k):
        recv(0, "xoa+", "xpa+", "xoa-", "xpa-", "xog+", "xpg+", "xog-", "xpg-")
        send("xf+", 0, G.at[:, 1, 0], G.at[:, 3, 0], XP)
        send("xf-", 0, G.at[:, 2, 1], G.at[:, 3, 1], XM)
        for n in (1, 2):
            send("qa", n, G.at[0, n, oc], Q.at[0, n], CO)
            send("qg", n, G.at[1, n, oc], Q.at[1, n], CO)

    def far_rows(k):
        recv(0, "xf+", "xf-")
        send("qa", 3, G.at[0, 3, oc], Q.at[0, 3], CO)
        send("qg", 3, G.at[1, 3, oc], Q.at[1, 3], CO)

    Y_ORDER = ((0, y2), (1, y2), (1, yp), (0, ym), (0, yp), (1, ym), (0, y), (1, y))
    Z_ORDER = tuple((oz, n) for n in range(4)) + tuple((zl, n) for n in range(4))

    def rows_in(ref, index, order):
        return jnp.concatenate(
            [ref[index + (pl.ds(pl.multiple_of((a * 4 + b) * BIN, BIN), BIN),)] for a, b in order], axis=0
        )

    def keep(raw, full, k, first, part):
        width = part.shape[1]
        raw[k, :, :, first:first + width] = part[:64].astype(BF).reshape(4, BIN, width)
        full[k, :, :, first:first + width] = part[64:].reshape(4, BIN, width)

    def product(a, b, own, par):
        return jnp.dot(a, own, preferred_element_type=F32) + jnp.dot(b, par, preferred_element_type=F32)

    def forward_y(k):
        n, j = src_of(k), k % NP
        h, w, _, _ = sizes(k)
        base = BASES[j]
        recv(n, "qa") if j == 0 else None
        recv(j, "wg", "wu") if n == 0 else None
        a, b = rows_in(G, (0, n, c), Y_ORDER), rows_in(Q, (0, n), Y_ORDER)
        cols = slice(base, base + h)
        keep(RY, FY, k, 0, product(a, b, wg[:, cols], pg[:, cols]))
        cols = slice(base, base + w - h)
        keep(RY, FY, k, h, product(a, b, wu[:, cols], pu[:, cols]))
        send("y1+", k, RY.at[k, 0, :, pl.ds(0, w)], y1.at[k, 0, :, pl.ds(0, w)], YP)
        send("y1-", k, RY.at[k, 1, :, pl.ds(0, w)], y1.at[k, 1, :, pl.ds(0, w)], YM)
        send("yo+", k, RY.at[k, 2, :, pl.ds(0, w)], yown.at[k, 1, :, pl.ds(0, w)], YP)
        send("yo-", k, RY.at[k, 3, :, pl.ds(0, w)], yown.at[k, 0, :, pl.ds(0, w)], YM)

    def forward_z(k):
        n, j = src_of(k), k % NP
        h, w, v, _ = sizes(k)
        base = BASES[j]
        a, b = rows_in(G, (0, n, c), Z_ORDER), rows_in(Q, (0, n), Z_ORDER)
        cols = slice(base + w - h, base + h)
        keep(RZ, FZ, k, 0, product(a, b, wu[:, cols], pu[:, cols]))
        recv(n, "qg") if j == 0 else None
        recv(j, "wd") if n == 0 else None
        a, b = rows_in(G, (1, n, c), Z_ORDER), rows_in(Q, (1, n), Z_ORDER)
        part = lax.dot_general(a, wd[base:base + h, :], NT, preferred_element_type=F32)
        part += lax.dot_general(b, pd[base:base + h, :], NT, preferred_element_type=F32)
        keep(RZ, FZ, k, 2 * h - w, part)
        send("z1", k, RZ.at[k, :, :, pl.ds(0, v)], z1.at[k, :, :, pl.ds(0, v)], ZL)

    def pass_y(k, half, name, to):
        w = sizes(k)[1]
        recv(k, "y1" + name)
        y1[k, half, :, :w] = (up32(y1[k, half, :, :w]) + FY[k, half, :, :w]).astype(BF)
        send("ya" + name, k, y1.at[k, half, :, pl.ds(0, w)], yacc.at[k, half, :, pl.ds(0, w)], to)

    def plus_y(k):
        pass_y(k, 0, "+", YP)

    def minus_y(k):
        pass_y(k, 1, "-", YM)

    def pass_z(k):
        _, _, v, u = sizes(k)
        recv(k, "z1")
        for row in (y2, yp, ym):
            z1[k, row, :, :v] = (up32(z1[k, row, :, :v]) + FZ[k, row, :, :v]).astype(BF)
        low, high = pl.ds(0, u), pl.ds(u, u)
        send("r1+", k, z1.at[k, y2, :, low], r1.at[k, 0, :, low], YP)
        send("r1-", k, z1.at[k, y2, :, high], r1.at[k, 1, :, low], YM)
        send("ro+", k, z1.at[k, yp, :, high], rown.at[k, 1, :, low], YP)
        send("ro-", k, z1.at[k, ym, :, low], rown.at[k, 0, :, low], YM)

    def cross_z(k):
        w = sizes(k)[1]
        recv(k, "yo+", "yo-", "ya+", "ya-")
        total = FY[k, 2 + oz, :, :w] + up32(yacc[k, oz, :, :w]) + up32(yown[k, oz, :, :w])
        ysend[k, :, :w] = total.astype(BF)
        send("yz", k, ysend.at[k, :, pl.ds(0, w)], yz.at[k, :, pl.ds(0, w)], ZL)

    def pass_r(k, half, name, row, to):
        u = sizes(k)[3]
        recv(k, "r1" + name)
        total = up32(r1[k, half, :, :u]) + up32(z1[k, row, :, half * u:half * u + u])
        r1[k, half, :, :u] = total.astype(BF)
        send("ra" + name, k, r1.at[k, half, :, pl.ds(0, u)], racc.at[k, half, :, pl.ds(0, u)], to)

    def plus_r(k):
        pass_r(k, 0, "+", yp, YP)

    def minus_r(k):
        pass_r(k, 1, "-", ym, YM)

    def finish(k):
        n = src_of(k)
        h, w, v, u = sizes(k)
        base = 3 * BASES[k % NP]
        recv(k, "yz", "ro+", "ro-", "ra+", "ra-")
        mine = zl * 4 + y
        F[:, :w] = (
            FY[k, 2 + zl, :, :w] + up32(yacc[k, zl, :, :w]) + up32(yown[k, zl, :, :w]) + up32(yz[k, :, :w])
        )
        for half in (0, 1):
            cols = slice(half * u, half * u + u)
            F[:, w + half * u:w + half * u + u] = (
                FZ[k, y, :, cols] + up32(z1[k, y, :, cols])
                + up32(racc[k, half, :, :u]) + up32(rown[k, half, :, :u])
            )
        gate, upper, back = F[:, :h], F[:, h:2 * h], F[:, 2 * h:3 * h]
        sigma = jax.nn.sigmoid(gate)
        swish = gate * sigma
        H[n, c, mine, :, base:base + h] = (swish * upper).astype(BF)
        H[n, c, mine, :, base + h:base + 2 * h] = (
            back * upper * sigma * (1.0 + gate * (1.0 - sigma))
        ).astype(BF)
        H[n, c, mine, :, base + 2 * h:base + 3 * h] = (back * swish).astype(BF)
        a = H.at[n, c, mine, :, y_cols(k)]
        b = H.at[n, c, mine, :, z_cols(k)]
        send("az", k, a, a, ZL)
        send("ay+", k, a, a, YP)
        send("ay-", k, a, a, YM)
        send("by+", k, b, b, YP)
        send("by-", k, b, b, YM)
        send("bz0", k, b, b, ZL)

    def move(name, k, plane, row, cols, to):
        part = H.at[src_of(k), c, plane * 4 + row, :, cols]
        send(name, k, part, part, to)

    def plus_b(k):
        recv(k, "by+")
        move("bf+", k, zl, ym, z_half(k, 0), YP)
        move("bz1", k, zl, ym, z_cols(k), ZL)

    def minus_b(k):
        recv(k, "by-")
        move("bf-", k, zl, yp, z_half(k, 1), YM)
        move("bz2", k, zl, yp, z_cols(k), ZL)

    def plane_a(k):
        recv(k, "az")
        move("ap+", k, oz, y, y_cols(k), YP)
        move("ap-", k, oz, y, y_cols(k), YM)

    def plus_a(k):
        recv(k, "ay+")
        move("af+", k, zl, ym, y_cols(k), YP)

    def far_b(k):
        recv(k, "bf+", "bf-")
        move("bz3", k, zl, y2, z_cols(k), ZL)

    def far_a(k):
        recv(k, "ap-")
        move("af-", k, oz, yp, y_cols(k), YM)

    def core_near(k):
        recv(k, "ay-")
        for n, row in enumerate((y, ym, yp)):
            move(f"ca{n}", k, zl, row, all_cols(k), CO)

    def core_far(k):
        recv(k, "af+", "af-", "ap+", "bz0", "bz1", "bz2", "bz3")
        part = H.at[src_of(k), c, pl.ds(oz * 4, 4), :, all_cols(k)]
        send("cc0", k, part, part, CO)
        move("cc1", k, zl, y2, all_cols(k), CO)

    def outputs(k):
        n, j = src_of(k), k % NP
        h = sizes(k)[0]
        base = 3 * BASES[j]
        hid = slice(BASES[j], BASES[j] + h)
        recv(k, "ca0", "ca1", "ca2", "cc0", "cc1")
        shape = (2, 2, 4, BIN, WIDTH)
        first = H[n, :, :, :, base:base + h].reshape(256, h)
        block = jnp.dot(first, wd[hid, :], preferred_element_type=F32).reshape(shape)
        first = H[n, :, :, :, base + h:base + 2 * h].reshape(256, h)
        inner = lax.dot_general(first, wg[:, hid], NT, preferred_element_type=F32)
        first = H[n, :, :, :, base + 2 * h:base + 3 * h].reshape(256, h)
        inner += lax.dot_general(first, wu[:, hid], NT, preferred_element_type=F32)
        inner = inner.reshape(shape)
        if j > 0:
            block += OB[n, :, :, :, :, :WIDTH]
            inner += OB[n, :, :, :, :, WIDTH:]
        OB[n, :, :, :, :, :WIDTH] = block
        OB[n, :, :, :, :, WIDTH:] = inner
        if j < NP - 1:
            return
        OL[n, :, :, :, :, :WIDTH] = block.astype(BF)
        OL[n, :, :, :, :, WIDTH:] = inner.astype(BF)
        if n < NS - 1:
            send("m+", n, OL.at[n, :, :, xp], rm.at[n], XP)
            send("m-", n, OL.at[n, :, :, xm], rp.at[n], XM)
            send("m2", n, OL.at[n, :, :, x2], r2.at[n], X2)
        else:
            send("dzx2", 0, OL.at[n, :, oh, x2], dr.at[6], dev(zh_=oh, x_=x2))
            send("dzx+", 0, OL.at[n, :, oh, xp], dr.at[4], dev(zh_=oh, x_=xp))
            send("dzx-", 0, OL.at[n, :, oh, xm], dr.at[5], dev(zh_=oh, x_=xm))
            send("dz", 0, OL.at[n, :, oh, x], dr.at[3], ZH)
            send("dx2", 0, OL.at[n, :, zh, x2], dr.at[2], X2)
            send("dx+", 0, OL.at[n, :, zh, xp], dr.at[0], XP)
            send("dx-", 0, OL.at[n, :, zh, xm], dr.at[1], XM)

    PLACES = ((0, 2, 1, 3), (2, 3, 0, 1), (3, 1, 2, 0), (1, 0, 3, 2))

    def earlier_sum(r, half):
        total = None
        for n, ref in zip(PLACES[r], (None, rm, rp, r2)):
            if n < NS - 1:
                part = OB[n, :, half, x] if ref is None else up32(ref[n, :, half])
                total = part if total is None else total + part
        return total

    def seq_exchange(k):
        for n in range(NS - 1):
            recv(n, "m+", "m-", "m2")
        for r in range(4):
            sz[r] = earlier_sum(r, oh).astype(BF)
        send("sz", 0, sz, rz, ZH)

    def seq_finish(k):
        recv(0, "dx+", "dx-", "dx2", "dz", "dzx+", "dzx-", "dzx2", "sz")
        late = {0: (2, 6), 1: (0, 4), 2: (3,), 3: (1, 5)}
        for r in range(4):
            total = earlier_sum(r, zh) + up32(rz[r])
            for j in late[r]:
                total += up32(dr[j])
            if r == 2:
                total += OB[NS - 1, :, zh, x]
            total = total.astype(BF)
            source = lax.rem(x + r, 4)
            block_out[:, source] = total[:, :, :WIDTH]
            input_out[:, source] = total[:, :, WIDTH:]

    def weight_grads(k):
        acts = G[0].reshape(1024, WIDTH)
        grads = G[1].reshape(1024, WIDTH)
        for j in range(NP):
            h = PARTS[j]
            for at in range(0, h, 512):
                width = min(512, h - at)
                to = pl.ds(BASES[j] + at, width)
                for place, out in ((1, tg), (2, tu)):
                    cols = pl.ds(3 * BASES[j] + place * h + at, width)
                    part = H[:, :, :, :, cols].reshape(1024, width)
                    part = lax.dot_general(acts, part, TN, preferred_element_type=F32)
                    out[:, to] = (part * (1.0 / 32.0)).astype(BF)
                part = H[:, :, :, :, pl.ds(3 * BASES[j] + at, width)].reshape(1024, width)
                part = lax.dot_general(part, grads, TN, preferred_element_type=F32)
                td[to, :] = (part * (1.0 / 32.0)).astype(BF)

    steps = (
        pack_acts, pack_grads, swap_weights, peer_acts, peer_grads, pass_on, far_rows,
        forward_y, forward_z, plus_y, minus_y, pass_z, cross_z, plus_r, minus_r, finish,
        plus_b, minus_b, plane_a, plus_a, far_b, far_a, core_near, core_far, outputs,
        seq_exchange, weight_grads, seq_finish,
    )
    for step in ORDER:
        steps[step // 10](step % 10)
    for cp in copies.values():
        cp.wait_send()


def run_mega(acts, grads, lengths, dest, mask, adv, gate, up, down):
    vm = pltpu.VMEM
    shape = jax.ShapeDtypeStruct
    rows = vm((2, 4, BIN, WIDTH), BF)
    wide, tall = vm((WIDTH, HID), BF), vm((HID, WIDTH), BF)
    hbm = pl.BlockSpec(memory_space=pl.ANY)
    whole = pl.BlockSpec(memory_space=vm)
    late = vm((NS - 1, 2, 2, BIN, 2 * WIDTH), BF)
    ybuf, zbuf = vm((NK, 2, BIN, MAXY), BF), vm((NK, 2, BIN, MAXZ // 2), BF)
    return pl.pallas_call(
        mega,
        out_shape=(rows, rows, wide, wide, tall),
        in_specs=[whole] * 6 + [hbm] * 3,
        out_specs=(whole,) * 5,
        scratch_shapes=[
            vm((WIDTH, HID), BF), vm((WIDTH, HID), BF), vm((HID, WIDTH), BF),
            vm((WIDTH, HID), BF), vm((WIDTH, HID), BF), vm((HID, WIDTH), BF),
            vm((2, NS, 2, 128, WIDTH), BF),
            vm((2, NS, 128, WIDTH), BF),
            vm((NK, 4, BIN, MAXY), BF), vm((NK, 4, BIN, MAXZ), BF),
            vm((NK, 4, BIN, MAXY), F32), vm((NK, 4, BIN, MAXZ), F32),
            vm((NS, 2, 8, BIN, ALL), BF),
            ybuf, ybuf, ybuf,
            vm((NK, BIN, MAXY), BF), vm((NK, BIN, MAXY), BF),
            vm((NK, 4, BIN, MAXZ), BF),
            zbuf, zbuf, zbuf,
            vm((BIN, 3 * max(PARTS)), F32),
            vm((NS, 2, 2, 4, BIN, 2 * WIDTH), F32),
            vm((NS, 2, 2, 4, BIN, 2 * WIDTH), BF),
            late, late, late,
            vm((4, 2, BIN, 2 * WIDTH), BF), vm((4, 2, BIN, 2 * WIDTH), BF),
            vm((7, 2, BIN, 2 * WIDTH), BF),
            pltpu.SemaphoreType.DMA((N_SEM,)),
            pltpu.SemaphoreType.DMA((N_SEM,)),
            pltpu.SemaphoreType.DMA((8,)),
        ],
        compiler_params=pltpu.CompilerParams(
            collective_id=0, has_side_effects=True, vmem_limit_bytes=54 * 2**20
        ),
        name="mega",
    )(acts, grads, lengths, dest, mask, adv, gate, up, down)


def widen_kernel(
    block, inner, wide_a, wide_b, tall, out_block, out_inner, out_a, out_b, out_c, stage, stage_tall, sem
):
    small = [
        pltpu.make_async_copy(block, out_block, sem.at[4]), pltpu.make_async_copy(inner, out_inner, sem.at[5])
    ]
    for cp in small:
        cp.start()
    pieces = [(src, dst, at, 128, stage) for src, dst in ((wide_a, out_a), (wide_b, out_b)) for at in range(0, WIDTH, 128)]
    pieces += [(tall, out_c, at, 480, stage_tall) for at in range(0, HID, 480)]
    flying = []
    for n, (src, dst, at, rows, held) in enumerate(pieces):
        slot = n % 4
        if n >= 4:
            flying[n - 4].wait()
        held[slot] = up32(src[at:at + rows, :])
        cp = pltpu.make_async_copy(held.at[slot], dst.at[pl.ds(at, rows)], sem.at[slot])
        cp.start()
        flying.append(cp)
    for cp in flying[-4:] + small:
        cp.wait()


def widen(block, inner, wide_a, wide_b, tall):
    shape = jax.ShapeDtypeStruct
    return pl.pallas_call(
        widen_kernel,
        out_shape=(
            shape(block.shape, BF), shape(inner.shape, BF),
            shape((WIDTH, HID), F32), shape((WIDTH, HID), F32), shape((HID, WIDTH), F32),
        ),
        in_specs=[pl.BlockSpec(memory_space=pltpu.VMEM)] * 5,
        out_specs=(pl.BlockSpec(memory_space=pl.ANY),) * 5,
        scratch_shapes=[
            pltpu.VMEM((4, 128, HID), F32), pltpu.VMEM((4, 480, WIDTH), F32), pltpu.SemaphoreType.DMA((6,)),
        ],
        compiler_params=pltpu.CompilerParams(vmem_limit_bytes=12 * 2**20),
        name="widen",
    )(block, inner, wide_a, wide_b, tall)


def per_device(
    rollout_acts, rollout_grads, lengths, destination, valid_mask, advantage,
    gate_weight, up_weight, down_weight,
):
    block, inner, gate_grad, up_grad, down_grad = run_mega(
        rollout_acts, rollout_grads, lengths, destination, valid_mask[None, :], advantage,
        gate_weight, up_weight, down_weight,
    )
    return widen(block.reshape(128, WIDTH), inner.reshape(128, WIDTH), gate_grad, up_grad, down_grad)


def solution(mesh):
    return jax.shard_map(
        per_device,
        mesh=mesh,
        in_specs=(
            P("seq", "tp"), P("seq", "tp"), P("seq", None), P("seq", None), P("seq"),
            P("seq", None), P("tp", "seq"), P("tp", "seq"), P("seq", "tp"),
        ),
        out_specs=(P("seq", "tp"), P("seq", "tp"), P("tp", "seq"), P("tp", "seq"), P("seq", "tp")),
        check_vma=False,
    )
```

```python
import jax
import jax.numpy as jnp
from jax import lax
from jax.experimental import pallas as pl
from jax.experimental.pallas import tpu as pltpu
from jax.sharding import PartitionSpec as P

BIN = 16
NS = 4
WIDTH = 512
HID = 1920
PARTS = (1024, 896)
YCOLS = (1792, 1664, 1792, 1664, 1280, 896, 1792, 1408)
ACOLS = (1792, 2176, 1536, 1664, 1792, 1152, 1024, 2432)
NP = len(PARTS)
NK = NS * NP
BASES = tuple(sum(PARTS[:j]) for j in range(NP))
ALL = 3 * HID
MAXY = max(YCOLS)
MAXZ = max(3 * PARTS[k % NP] - w for k, w in enumerate(YCOLS))
BF = jnp.bfloat16
F32 = jnp.float32
MESH = pl.DeviceIdType.MESH
NT = (((1,), (1,)), ((), ()))
TN = (((0,), (0,)), ((), ()))

ORDER = (
    0, 10, 20, 30, 40, 70, 80, 71, 81, 50, 100, 90, 72, 82, 110, 73, 83, 120, 111, 74, 60, 84, 101, 130,
    140, 112, 102, 91, 131, 141, 103, 92, 93, 104, 113, 94, 132, 150, 121, 142, 122, 75, 114, 85, 180, 123,
    124, 133, 143, 190, 151, 170, 152, 160, 220, 105, 134, 144, 95, 210, 115, 171, 191, 153, 161, 172, 221,
    181, 200, 162, 154, 182, 192, 222, 125, 135, 145, 173, 193, 183, 163, 201, 223, 211, 202, 230, 174, 194,
    212, 164, 184, 224, 240, 213, 155, 231, 76, 232, 203, 86, 214, 77, 204, 185, 87, 241, 233, 175, 165,
    106, 195, 225, 96, 242, 116, 234, 107, 97, 243, 205, 215, 244, 117, 126, 136, 146, 127, 235, 137, 147,
    156, 157, 245, 186, 196, 166, 176, 226, 187, 177, 167, 216, 197, 227, 206, 217, 207, 250, 236, 237, 246,
    247, 260, 270,
)

SEQ_NAMES = (
    "zha", "zhg", "xoa+", "xoa-", "xog+", "xog-", "xpa+", "xpa-", "xpg+", "xpg-", "xf+", "xf-",
    "sz",
)
LATE_NAMES = ("dx+", "dx-", "dx2", "dz", "dzx+", "dzx-", "dzx2")
PIECE_NAMES = (
    "y1+", "y1-", "yo+", "yo-", "ya+", "ya-", "yz",
    "z1", "r1+", "r1-", "ro+", "ro-", "ra+", "ra-",
    "az", "ay+", "ay-", "by+", "by-", "bz0", "ap+", "ap-", "bf+", "bf-",
    "bz1", "bz2", "af+", "af-", "bz3", "ca0", "ca1", "ca2", "cc0", "cc1",
)
SEM = {}
for _n in SEQ_NAMES:
    SEM[(_n, 0)] = len(SEM)
for _k in range(2):
    for _n in LATE_NAMES:
        SEM[(_n, _k)] = len(SEM)
for _k in range(NP):
    for _n in ("wg", "wu", "wd"):
        SEM[(_n, _k)] = len(SEM)
for _k in range(NS):
    for _n in ("qa", "qg", "m+", "m-", "m2"):
        SEM[(_n, _k)] = len(SEM)
for _k in range(NK):
    for _n in PIECE_NAMES:
        SEM[(_n, _k)] = len(SEM)
N_SEM = len(SEM)


def up32(value):
    return value.astype(F32)


def routing(lengths, destination, advantage, mask):
    diagonal = lax.broadcasted_iota(jnp.int32, (16, 16), 0) == lax.broadcasted_iota(jnp.int32, (16, 16), 1)

    def column(row):
        return jnp.sum(jnp.where(diagonal, row, jnp.zeros_like(row)), axis=1, keepdims=True)

    resp = lax.broadcasted_iota(jnp.int32, (16, 256), 0)
    row = lax.broadcasted_iota(jnp.int32, (16, 256), 1)
    of_row = row // BIN
    mine = of_row == resp

    def spread(col):
        return jnp.sum(jnp.where(mine, col, jnp.zeros_like(col)), axis=0, keepdims=True)

    len_col, dest_col = column(lengths), column(destination)
    len_row, dest_row = spread(len_col), spread(dest_col)
    before = (dest_col == dest_row) & (resp < of_row)
    offset = jnp.sum(jnp.where(before, len_col, 0), axis=0, keepdims=True)
    within = lax.rem(row[:1], BIN)
    slot = jnp.where(within < len_row, dest_row * BIN + offset + within, -1)
    hot = lax.broadcasted_iota(jnp.int32, (128, 256), 0) == slot
    weight = spread(column(advantage)) * mask.astype(F32)
    weight = jnp.sum(jnp.where(hot, weight, 0.0), axis=1, keepdims=True)
    return jnp.where(hot, 1.0, 0.0).astype(BF), weight


def mega(
    acts_hbm, grads_hbm, lengths_ref, dest_ref, mask_ref, adv_ref, gate_hbm, up_hbm, down_hbm,
    block_out, input_out, tg, tu, td,
    acts_ref, grads_ref, wg, wu, wd, pg, pu, pd, G, Q, RY, RZ, FY, FZ, H,
    y1, yown, yacc, ysend, yz, z1, r1, rown, racc, F,
    OB, OL, rm, rp, r2, sz, rz, dr,
    ssem, rsem, lsem,
):
    s = lax.axis_index("seq")
    t = lax.axis_index("tp")
    zh, x = s // 4, lax.rem(s, 4)
    zl, y, c = t // 8, lax.rem(t // 2, 4), lax.rem(t, 2)
    oz, oc, oh = 1 - zl, 1 - c, 1 - zh
    yp, ym, y2 = lax.rem(y + 1, 4), lax.rem(y + 3, 4), lax.rem(y + 2, 4)
    xp, xm, x2 = lax.rem(x + 1, 4), lax.rem(x + 3, 4), lax.rem(x + 2, 4)

    def dev(zh_=zh, x_=x, zl_=zl, y_=y, c_=c):
        return (zh_ * 4 + x_, zl_ * 8 + y_ * 2 + c_)

    XP, XM, X2 = dev(x_=xp), dev(x_=xm), dev(x_=x2)
    YP, YM = dev(y_=yp), dev(y_=ym)
    ZL, ZH, CO = dev(zl_=oz), dev(zh_=oh), dev(c_=oc)

    copies = {}

    def send(name, k, src, dst, to):
        i = SEM[(name, k)]
        cp = pltpu.make_async_remote_copy(
            src_ref=src, dst_ref=dst, send_sem=ssem.at[i], recv_sem=rsem.at[i],
            device_id=to, device_id_type=MESH,
        )
        cp.start()
        copies[(name, k)] = cp

    def recv(k, *names):
        for name in names:
            copies[(name, k)].wait_recv()

    local = []

    def local_copy(src, dst):
        cp = pltpu.make_async_copy(src, dst, lsem.at[len(local)])
        cp.start()
        local.append(cp)
        return cp

    def src_of(k):
        return k // NP

    def hid_of(k):
        return pl.ds(BASES[k % NP], PARTS[k % NP])

    def sizes(k):
        h, w = PARTS[k % NP], YCOLS[k]
        return h, w, 3 * h - w, (3 * h - w) // 2

    def all_cols(k):
        return pl.ds(3 * BASES[k % NP], 3 * PARTS[k % NP])

    def y_cols(k):
        return pl.ds(3 * BASES[k % NP], ACOLS[k])

    def z_cols(k):
        return pl.ds(3 * BASES[k % NP] + ACOLS[k], 3 * PARTS[k % NP] - ACOLS[k])

    def z_half(k, half):
        width = (3 * PARTS[k % NP] - ACOLS[k]) // 2
        return pl.ds(3 * BASES[k % NP] + ACOLS[k] + half * width, width)

    barrier = pltpu.get_barrier_semaphore()
    peers = [XP, XM, YP, YM, ZL, ZH, CO, X2]
    for peer in peers:
        pl.semaphore_signal(barrier, inc=1, device_id=peer, device_id_type=MESH)
    raw = [local_copy(acts_hbm, acts_ref), local_copy(grads_hbm, grads_ref)]
    loads = [local_copy(gate_hbm, wg), local_copy(up_hbm, wu), local_copy(down_hbm, wd)]
    hot, weight = routing(lengths_ref[...], dest_ref[...], adv_ref[...], mask_ref[...])

    def spread_own(arr, n):
        send("zh" + n, 0, G.at[arr, 0, zh], G.at[arr, 0, zh], ZH)
        send("xo" + n + "+", 0, G.at[arr, 0, zh], G.at[arr, 1, zh], XP)
        send("xo" + n + "-", 0, G.at[arr, 0, zh], G.at[arr, 2, zh], XM)

    def spread_peer(arr, n):
        recv(0, "zh" + n)
        send("q" + n, 0, G.at[arr, 0, oc], Q.at[arr, 0], CO)
        send("xp" + n + "+", 0, G.at[arr, 0, oh], G.at[arr, 1, oh], XP)
        send("xp" + n + "-", 0, G.at[arr, 0, oh], G.at[arr, 2, oh], XM)

    def pack_acts(k):
        raw[0].wait()
        G[0, 0, zh] = jnp.dot(hot, acts_ref[...], preferred_element_type=F32).astype(BF)
        pl.semaphore_wait(barrier, len(peers))
        spread_own(0, "a")

    def pack_grads(k):
        raw[1].wait()
        packed = jnp.dot(hot, grads_ref[...], preferred_element_type=F32)
        G[1, 0, zh] = (packed * weight).astype(BF)
        spread_own(1, "g")

    def swap_weights(k):
        for cp in loads:
            cp.wait()
        for j in range(NP):
            hid = hid_of(j)
            send("wg", j, wg.at[:, hid], pg.at[:, hid], CO)
            send("wu", j, wu.at[:, hid], pu.at[:, hid], CO)
            send("wd", j, wd.at[hid], pd.at[hid], CO)

    def peer_acts(k):
        spread_peer(0, "a")

    def peer_grads(k):
        spread_peer(1, "g")

    def pass_on(k):
        recv(0, "xoa+", "xpa+", "xoa-", "xpa-", "xog+", "xpg+", "xog-", "xpg-")
        send("xf+", 0, G.at[:, 1, 0], G.at[:, 3, 0], XP)
        send("xf-", 0, G.at[:, 2, 1], G.at[:, 3, 1], XM)
        for n in (1, 2):
            send("qa", n, G.at[0, n, oc], Q.at[0, n], CO)
            send("qg", n, G.at[1, n, oc], Q.at[1, n], CO)

    def far_rows(k):
        recv(0, "xf+", "xf-")
        send("qa", 3, G.at[0, 3, oc], Q.at[0, 3], CO)
        send("qg", 3, G.at[1, 3, oc], Q.at[1, 3], CO)

    Y_ORDER = ((0, y2), (1, y2), (1, yp), (0, ym), (0, yp), (1, ym), (0, y), (1, y))
    Z_ORDER = tuple((oz, n) for n in range(4)) + tuple((zl, n) for n in range(4))

    def rows_in(ref, index, order):
        return jnp.concatenate(
            [ref[index + (pl.ds(pl.multiple_of((a * 4 + b) * BIN, BIN), BIN),)] for a, b in order], axis=0
        )

    def keep(raw, full, k, first, part):
        width = part.shape[1]
        raw[k, :, :, first:first + width] = part[:64].astype(BF).reshape(4, BIN, width)
        full[k, :, :, first:first + width] = part[64:].reshape(4, BIN, width)

    def product(a, b, own, par):
        return jnp.dot(a, own, preferred_element_type=F32) + jnp.dot(b, par, preferred_element_type=F32)

    def forward_y(k):
        n, j = src_of(k), k % NP
        h, w, _, _ = sizes(k)
        base = BASES[j]
        recv(n, "qa") if j == 0 else None
        recv(j, "wg", "wu") if n == 0 else None
        a, b = rows_in(G, (0, n, c), Y_ORDER), rows_in(Q, (0, n), Y_ORDER)
        cols = slice(base, base + h)
        keep(RY, FY, k, 0, product(a, b, wg[:, cols], pg[:, cols]))
        if w > h:
            cols = slice(base, base + w - h)
            keep(RY, FY, k, h, product(a, b, wu[:, cols], pu[:, cols]))
        send("y1+", k, RY.at[k, 0, :, pl.ds(0, w)], y1.at[k, 0, :, pl.ds(0, w)], YP)
        send("y1-", k, RY.at[k, 1, :, pl.ds(0, w)], y1.at[k, 1, :, pl.ds(0, w)], YM)
        send("yo+", k, RY.at[k, 2, :, pl.ds(0, w)], yown.at[k, 1, :, pl.ds(0, w)], YP)
        send("yo-", k, RY.at[k, 3, :, pl.ds(0, w)], yown.at[k, 0, :, pl.ds(0, w)], YM)

    def forward_z(k):
        n, j = src_of(k), k % NP
        h, w, v, _ = sizes(k)
        base = BASES[j]
        a, b = rows_in(G, (0, n, c), Z_ORDER), rows_in(Q, (0, n), Z_ORDER)
        cols = slice(base + w - h, base + h)
        keep(RZ, FZ, k, 0, product(a, b, wu[:, cols], pu[:, cols]))
        recv(n, "qg") if j == 0 else None
        recv(j, "wd") if n == 0 else None
        a, b = rows_in(G, (1, n, c), Z_ORDER), rows_in(Q, (1, n), Z_ORDER)
        part = lax.dot_general(a, wd[base:base + h, :], NT, preferred_element_type=F32)
        part += lax.dot_general(b, pd[base:base + h, :], NT, preferred_element_type=F32)
        keep(RZ, FZ, k, 2 * h - w, part)
        send("z1", k, RZ.at[k, :, :, pl.ds(0, v)], z1.at[k, :, :, pl.ds(0, v)], ZL)

    def pass_y(k, half, name, to):
        w = sizes(k)[1]
        recv(k, "y1" + name)
        y1[k, half, :, :w] = (up32(y1[k, half, :, :w]) + FY[k, half, :, :w]).astype(BF)
        send("ya" + name, k, y1.at[k, half, :, pl.ds(0, w)], yacc.at[k, half, :, pl.ds(0, w)], to)

    def plus_y(k):
        pass_y(k, 0, "+", YP)

    def minus_y(k):
        pass_y(k, 1, "-", YM)

    def pass_z(k):
        _, _, v, u = sizes(k)
        recv(k, "z1")
        for row in (y2, yp, ym):
            z1[k, row, :, :v] = (up32(z1[k, row, :, :v]) + FZ[k, row, :, :v]).astype(BF)
        low, high = pl.ds(0, u), pl.ds(u, u)
        send("r1+", k, z1.at[k, y2, :, low], r1.at[k, 0, :, low], YP)
        send("r1-", k, z1.at[k, y2, :, high], r1.at[k, 1, :, low], YM)
        send("ro+", k, z1.at[k, yp, :, high], rown.at[k, 1, :, low], YP)
        send("ro-", k, z1.at[k, ym, :, low], rown.at[k, 0, :, low], YM)

    def cross_z(k):
        w = sizes(k)[1]
        recv(k, "yo+", "yo-", "ya+", "ya-")
        total = FY[k, 2 + oz, :, :w] + up32(yacc[k, oz, :, :w]) + up32(yown[k, oz, :, :w])
        ysend[k, :, :w] = total.astype(BF)
        send("yz", k, ysend.at[k, :, pl.ds(0, w)], yz.at[k, :, pl.ds(0, w)], ZL)

    def pass_r(k, half, name, row, to):
        u = sizes(k)[3]
        recv(k, "r1" + name)
        total = up32(r1[k, half, :, :u]) + up32(z1[k, row, :, half * u:half * u + u])
        r1[k, half, :, :u] = total.astype(BF)
        send("ra" + name, k, r1.at[k, half, :, pl.ds(0, u)], racc.at[k, half, :, pl.ds(0, u)], to)

    def plus_r(k):
        pass_r(k, 0, "+", yp, YP)

    def minus_r(k):
        pass_r(k, 1, "-", ym, YM)

    def finish(k):
        n = src_of(k)
        h, w, v, u = sizes(k)
        base = 3 * BASES[k % NP]
        recv(k, "yz", "ro+", "ro-", "ra+", "ra-")
        mine = zl * 4 + y
        F[:, :w] = (
            FY[k, 2 + zl, :, :w] + up32(yacc[k, zl, :, :w]) + up32(yown[k, zl, :, :w]) + up32(yz[k, :, :w])
        )
        for half in (0, 1):
            cols = slice(half * u, half * u + u)
            F[:, w + half * u:w + half * u + u] = (
                FZ[k, y, :, cols] + up32(z1[k, y, :, cols])
                + up32(racc[k, half, :, :u]) + up32(rown[k, half, :, :u])
            )
        gate, upper, back = F[:, :h], F[:, h:2 * h], F[:, 2 * h:3 * h]
        sigma = jax.nn.sigmoid(gate)
        swish = gate * sigma
        H[n, c, mine, :, base:base + h] = (swish * upper).astype(BF)
        H[n, c, mine, :, base + h:base + 2 * h] = (
            back * upper * sigma * (1.0 + gate * (1.0 - sigma))
        ).astype(BF)
        H[n, c, mine, :, base + 2 * h:base + 3 * h] = (back * swish).astype(BF)
        a = H.at[n, c, mine, :, y_cols(k)]
        b = H.at[n, c, mine, :, z_cols(k)]
        send("az", k, a, a, ZL)
        send("ay+", k, a, a, YP)
        send("ay-", k, a, a, YM)
        send("by+", k, b, b, YP)
        send("by-", k, b, b, YM)
        send("bz0", k, b, b, ZL)

    def move(name, k, plane, row, cols, to):
        part = H.at[src_of(k), c, plane * 4 + row, :, cols]
        send(name, k, part, part, to)

    def plus_b(k):
        recv(k, "by+")
        move("bf+", k, zl, ym, z_half(k, 0), YP)
        move("bz1", k, zl, ym, z_cols(k), ZL)

    def minus_b(k):
        recv(k, "by-")
        move("bf-", k, zl, yp, z_half(k, 1), YM)
        move("bz2", k, zl, yp, z_cols(k), ZL)

    def plane_a(k):
        recv(k, "az")
        move("ap+", k, oz, y, y_cols(k), YP)
        move("ap-", k, oz, y, y_cols(k), YM)

    def plus_a(k):
        recv(k, "ay+")
        move("af+", k, zl, ym, y_cols(k), YP)

    def far_b(k):
        recv(k, "bf+", "bf-")
        move("bz3", k, zl, y2, z_cols(k), ZL)

    def far_a(k):
        recv(k, "ap-")
        move("af-", k, oz, yp, y_cols(k), YM)

    def core_near(k):
        recv(k, "ay-")
        for n, row in enumerate((y, ym, yp)):
            move(f"ca{n}", k, zl, row, all_cols(k), CO)

    def core_far(k):
        recv(k, "af+", "af-", "ap+", "bz0", "bz1", "bz2", "bz3")
        part = H.at[src_of(k), c, pl.ds(oz * 4, 4), :, all_cols(k)]
        send("cc0", k, part, part, CO)
        move("cc1", k, zl, y2, all_cols(k), CO)

    def outputs(k):
        n, j = src_of(k), k % NP
        h = sizes(k)[0]
        base = 3 * BASES[j]
        hid = slice(BASES[j], BASES[j] + h)
        recv(k, "ca0", "ca1", "ca2", "cc0", "cc1")
        shape = (2, 2, 4, BIN, WIDTH)
        first = H[n, :, :, :, base:base + h].reshape(256, h)
        block = jnp.dot(first, wd[hid, :], preferred_element_type=F32).reshape(shape)
        if j > 0:
            block += OB[n, :, :, :, :, :WIDTH]
        OB[n, :, :, :, :, :WIDTH] = block
        if j == NP - 1:
            OL[n, :, :, :, :, :WIDTH] = block.astype(BF)
            if n == NS - 1:
                late_sends(0)
        first = H[n, :, :, :, base + h:base + 2 * h].reshape(256, h)
        inner = lax.dot_general(first, wg[:, hid], NT, preferred_element_type=F32)
        first = H[n, :, :, :, base + 2 * h:base + 3 * h].reshape(256, h)
        inner += lax.dot_general(first, wu[:, hid], NT, preferred_element_type=F32)
        inner = inner.reshape(shape)
        if j > 0:
            inner += OB[n, :, :, :, :, WIDTH:]
        OB[n, :, :, :, :, WIDTH:] = inner
        if j < NP - 1:
            return
        OL[n, :, :, :, :, WIDTH:] = inner.astype(BF)
        if n < NS - 1:
            send("m+", n, OL.at[n, :, :, xp], rm.at[n], XP)
            send("m-", n, OL.at[n, :, :, xm], rp.at[n], XM)
            send("m2", n, OL.at[n, :, :, x2], r2.at[n], X2)
        else:
            late_sends(1)

    def late_sends(side):
        cols = pl.ds(side * WIDTH, WIDTH)
        for name, slot, a, b in (
            ("dzx2", 6, oh, x2), ("dzx+", 4, oh, xp), ("dzx-", 5, oh, xm), ("dz", 3, oh, x),
            ("dx2", 2, zh, x2), ("dx+", 0, zh, xp), ("dx-", 1, zh, xm),
        ):
            send(name, side, OL.at[NS - 1, :, a, b, :, cols], dr.at[slot, :, :, cols], dev(zh_=a, x_=b))

    PLACES = ((0, 2, 1, 3), (2, 3, 0, 1), (3, 1, 2, 0), (1, 0, 3, 2))

    def earlier_sum(r, half):
        total = None
        for n, ref in zip(PLACES[r], (None, rm, rp, r2)):
            if n < NS - 1:
                part = OB[n, :, half, x] if ref is None else up32(ref[n, :, half])
                total = part if total is None else total + part
        return total

    def seq_exchange(k):
        for n in range(NS - 1):
            recv(n, "m+", "m-", "m2")
        for r in range(4):
            sz[r] = earlier_sum(r, oh).astype(BF)
        send("sz", 0, sz, rz, ZH)

    def seq_finish(k):
        recv(0, "sz")
        for side in (0, 1):
            recv(side, *LATE_NAMES)
        late = {0: (2, 6), 1: (0, 4), 2: (3,), 3: (1, 5)}
        for r in range(4):
            total = earlier_sum(r, zh) + up32(rz[r])
            for j in late[r]:
                total += up32(dr[j])
            if r == 2:
                total += OB[NS - 1, :, zh, x]
            total = total.astype(BF)
            source = lax.rem(x + r, 4)
            block_out[:, source] = total[:, :, :WIDTH]
            input_out[:, source] = total[:, :, WIDTH:]

    def weight_grads(k):
        acts = G[0].reshape(1024, WIDTH)
        grads = G[1].reshape(1024, WIDTH)
        for j in range(NP):
            h = PARTS[j]
            for at in range(0, h, 512):
                width = min(512, h - at)
                to = pl.ds(BASES[j] + at, width)
                for place, out in ((1, tg), (2, tu)):
                    cols = pl.ds(3 * BASES[j] + place * h + at, width)
                    part = H[:, :, :, :, cols].reshape(1024, width)
                    part = lax.dot_general(acts, part, TN, preferred_element_type=F32)
                    out[:, to] = (part * (1.0 / 32.0)).astype(BF)
                part = H[:, :, :, :, pl.ds(3 * BASES[j] + at, width)].reshape(1024, width)
                part = lax.dot_general(part, grads, TN, preferred_element_type=F32)
                td[to, :] = (part * (1.0 / 32.0)).astype(BF)

    steps = (
        pack_acts, pack_grads, swap_weights, peer_acts, peer_grads, pass_on, far_rows,
        forward_y, forward_z, plus_y, minus_y, pass_z, cross_z, plus_r, minus_r, finish,
        plus_b, minus_b, plane_a, plus_a, far_b, far_a, core_near, core_far, outputs,
        seq_exchange, weight_grads, seq_finish,
    )
    for step in ORDER:
        steps[step // 10](step % 10)
    for cp in copies.values():
        cp.wait_send()


def run_mega(acts, grads, lengths, dest, mask, adv, gate, up, down):
    vm = pltpu.VMEM
    shape = jax.ShapeDtypeStruct
    rows = vm((2, 4, BIN, WIDTH), BF)
    wide, tall = vm((WIDTH, HID), BF), vm((HID, WIDTH), BF)
    hbm = pl.BlockSpec(memory_space=pl.ANY)
    whole = pl.BlockSpec(memory_space=vm)
    late = vm((NS - 1, 2, 2, BIN, 2 * WIDTH), BF)
    ybuf, zbuf = vm((NK, 2, BIN, MAXY), BF), vm((NK, 2, BIN, MAXZ // 2), BF)
    return pl.pallas_call(
        mega,
        out_shape=(rows, rows, wide, wide, tall),
        in_specs=[hbm] * 2 + [whole] * 4 + [hbm] * 3,
        out_specs=(whole,) * 5,
        scratch_shapes=[
            vm((2 * 128, WIDTH), BF), vm((2 * 128, WIDTH), BF),
            vm((WIDTH, HID), BF), vm((WIDTH, HID), BF), vm((HID, WIDTH), BF),
            vm((WIDTH, HID), BF), vm((WIDTH, HID), BF), vm((HID, WIDTH), BF),
            vm((2, NS, 2, 128, WIDTH), BF),
            vm((2, NS, 128, WIDTH), BF),
            vm((NK, 4, BIN, MAXY), BF), vm((NK, 4, BIN, MAXZ), BF),
            vm((NK, 4, BIN, MAXY), F32), vm((NK, 4, BIN, MAXZ), F32),
            vm((NS, 2, 8, BIN, ALL), BF),
            ybuf, ybuf, ybuf,
            vm((NK, BIN, MAXY), BF), vm((NK, BIN, MAXY), BF),
            vm((NK, 4, BIN, MAXZ), BF),
            zbuf, zbuf, zbuf,
            vm((BIN, 3 * max(PARTS)), F32),
            vm((NS, 2, 2, 4, BIN, 2 * WIDTH), F32),
            vm((NS, 2, 2, 4, BIN, 2 * WIDTH), BF),
            late, late, late,
            vm((4, 2, BIN, 2 * WIDTH), BF), vm((4, 2, BIN, 2 * WIDTH), BF),
            vm((7, 2, BIN, 2 * WIDTH), BF),
            pltpu.SemaphoreType.DMA((N_SEM,)),
            pltpu.SemaphoreType.DMA((N_SEM,)),
            pltpu.SemaphoreType.DMA((8,)),
        ],
        compiler_params=pltpu.CompilerParams(
            collective_id=0, has_side_effects=True, vmem_limit_bytes=54 * 2**20
        ),
        name="mega",
    )(acts, grads, lengths, dest, mask, adv, gate, up, down)


def widen_kernel(
    block, inner, wide_a, wide_b, tall, out_block, out_inner, out_a, out_b, out_c, stage, stage_tall, sem
):
    small = [
        pltpu.make_async_copy(block, out_block, sem.at[4]), pltpu.make_async_copy(inner, out_inner, sem.at[5])
    ]
    for cp in small:
        cp.start()
    pieces = [(src, dst, at, 128, stage) for src, dst in ((wide_a, out_a), (wide_b, out_b)) for at in range(0, WIDTH, 128)]
    pieces += [(tall, out_c, at, 480, stage_tall) for at in range(0, HID, 480)]
    flying = []
    for n, (src, dst, at, rows, held) in enumerate(pieces):
        slot = n % 4
        if n >= 4:
            flying[n - 4].wait()
        held[slot] = up32(src[at:at + rows, :])
        cp = pltpu.make_async_copy(held.at[slot], dst.at[pl.ds(at, rows)], sem.at[slot])
        cp.start()
        flying.append(cp)
    for cp in flying[-4:] + small:
        cp.wait()


def widen(block, inner, wide_a, wide_b, tall):
    shape = jax.ShapeDtypeStruct
    return pl.pallas_call(
        widen_kernel,
        out_shape=(
            shape(block.shape, BF), shape(inner.shape, BF),
            shape((WIDTH, HID), F32), shape((WIDTH, HID), F32), shape((HID, WIDTH), F32),
        ),
        in_specs=[pl.BlockSpec(memory_space=pltpu.VMEM)] * 5,
        out_specs=(pl.BlockSpec(memory_space=pl.ANY),) * 5,
        scratch_shapes=[
            pltpu.VMEM((4, 128, HID), F32), pltpu.VMEM((4, 480, WIDTH), F32), pltpu.SemaphoreType.DMA((6,)),
        ],
        compiler_params=pltpu.CompilerParams(vmem_limit_bytes=12 * 2**20),
        name="widen",
    )(block, inner, wide_a, wide_b, tall)


def per_device(
    rollout_acts, rollout_grads, lengths, destination, valid_mask, advantage,
    gate_weight, up_weight, down_weight,
):
    block, inner, gate_grad, up_grad, down_grad = run_mega(
        rollout_acts, rollout_grads, lengths, destination, valid_mask[None, :], advantage,
        gate_weight, up_weight, down_weight,
    )
    return widen(block.reshape(128, WIDTH), inner.reshape(128, WIDTH), gate_grad, up_grad, down_grad)


def solution(mesh):
    return jax.shard_map(
        per_device,
        mesh=mesh,
        in_specs=(
            P("seq", "tp"), P("seq", "tp"), P("seq", None), P("seq", None), P("seq"),
            P("seq", None), P("tp", "seq"), P("tp", "seq"), P("seq", "tp"),
        ),
        out_specs=(P("seq", "tp"), P("seq", "tp"), P("tp", "seq"), P("tp", "seq"), P("seq", "tp")),
        check_vma=False,
    )
```

```python
import jax
import jax.numpy as jnp
from jax import lax
from jax.experimental import pallas as pl
from jax.experimental.pallas import tpu as pltpu
from jax.sharding import PartitionSpec as P

BIN = 16
NS = 4
WIDTH = 512
HID = 1920
PARTS = (1024, 896)
YCOLS = (1792, 1152, 1792, 1664, 1792, 1152, 1792, 896)
ACOLS = (1792, 1664, 2304, 1152, 2048, 1664, 1024, 2176)
NP = len(PARTS)
NK = NS * NP
BASES = tuple(sum(PARTS[:j]) for j in range(NP))
ALL = 3 * HID
MAXY = max(YCOLS)
MAXZ = max(3 * PARTS[k % NP] - w for k, w in enumerate(YCOLS))
BF = jnp.bfloat16
F32 = jnp.float32
MESH = pl.DeviceIdType.MESH
NT = (((1,), (1,)), ((), ()))
TN = (((0,), (0,)), ((), ()))

ORDER = (
    0, 10, 20, 30, 40, 70, 80, 71, 50, 90, 100, 81, 72, 101, 91, 82, 110, 73, 120, 102, 92, 83, 74, 60, 130,
    140, 121, 111, 103, 93, 84, 75, 122, 112, 94, 104, 85, 150, 131, 141, 113, 123, 95, 105, 132, 142, 114,
    124, 190, 160, 170, 220, 151, 133, 143, 125, 152, 180, 134, 144, 115, 200, 171, 191, 161, 221, 153, 172,
    192, 162, 210, 181, 222, 145, 154, 135, 182, 173, 201, 193, 230, 163, 211, 183, 223, 240, 202, 174, 184,
    212, 194, 164, 224, 155, 231, 213, 76, 203, 214, 86, 77, 232, 185, 87, 241, 233, 204, 195, 175, 165,
    106, 225, 242, 96, 116, 97, 107, 243, 215, 205, 117, 234, 126, 136, 146, 127, 235, 137, 147, 244, 156,
    157, 245, 186, 196, 166, 176, 226, 187, 167, 197, 177, 216, 227, 206, 217, 207, 250, 236, 237, 246, 247,
    260, 270,
)

SEQ_NAMES = (
    "zha", "zhg", "xoa+", "xoa-", "xog+", "xog-", "xpa+", "xpa-", "xpg+", "xpg-", "xf+", "xf-",
    "sz",
)
LATE_NAMES = ("dx+", "dx-", "dx2", "dz", "dzx+", "dzx-", "dzx2")
PIECE_NAMES = (
    "y1+", "y1-", "yo+", "yo-", "ya+", "ya-", "yz",
    "z1", "r1+", "r1-", "ro+", "ro-", "ra+", "ra-",
    "az", "ay+", "ay-", "by+", "by-", "bz0", "ap+", "ap-", "bf+", "bf-",
    "bz1", "bz2", "af+", "af-", "bz3", "ca0", "ca1", "ca2", "cc0", "cc1",
)
SEM = {}
for _n in SEQ_NAMES:
    SEM[(_n, 0)] = len(SEM)
for _k in range(2):
    for _n in LATE_NAMES:
        SEM[(_n, _k)] = len(SEM)
for _k in range(NP):
    for _n in ("wg", "wu", "wd"):
        SEM[(_n, _k)] = len(SEM)
for _k in range(NS):
    for _n in ("qa", "qg", "m+", "m-", "m2"):
        SEM[(_n, _k)] = len(SEM)
for _k in range(NK):
    for _n in PIECE_NAMES:
        SEM[(_n, _k)] = len(SEM)
N_SEM = len(SEM)


def up32(value):
    return value.astype(F32)


def routing(lengths, destination, advantage, mask):
    diagonal = lax.broadcasted_iota(jnp.int32, (16, 16), 0) == lax.broadcasted_iota(jnp.int32, (16, 16), 1)

    def column(row):
        return jnp.sum(jnp.where(diagonal, row, jnp.zeros_like(row)), axis=1, keepdims=True)

    resp = lax.broadcasted_iota(jnp.int32, (16, 256), 0)
    row = lax.broadcasted_iota(jnp.int32, (16, 256), 1)
    of_row = row // BIN
    mine = of_row == resp

    def spread(col):
        return jnp.sum(jnp.where(mine, col, jnp.zeros_like(col)), axis=0, keepdims=True)

    len_col, dest_col = column(lengths), column(destination)
    len_row, dest_row = spread(len_col), spread(dest_col)
    before = (dest_col == dest_row) & (resp < of_row)
    offset = jnp.sum(jnp.where(before, len_col, 0), axis=0, keepdims=True)
    within = lax.rem(row[:1], BIN)
    slot = jnp.where(within < len_row, dest_row * BIN + offset + within, -1)
    hot = lax.broadcasted_iota(jnp.int32, (128, 256), 0) == slot
    weight = spread(column(advantage)) * mask.astype(F32)
    weight = jnp.sum(jnp.where(hot, weight, 0.0), axis=1, keepdims=True)
    return jnp.where(hot, 1.0, 0.0).astype(BF), weight


def mega(
    acts_hbm, grads_hbm, lengths_ref, dest_ref, mask_ref, adv_ref, gate_hbm, up_hbm, down_hbm,
    block_out, input_out, tg, tu, td,
    acts_ref, grads_ref, wg, wu, wd, pg, pu, pd, G, Q, RY, RZ, FY, FZ, H,
    y1, yown, yacc, ysend, yz, z1, r1, rown, racc, F,
    OB, OL, rm, rp, r2, sz, rz, dr,
    ssem, rsem, lsem,
):
    s = lax.axis_index("seq")
    t = lax.axis_index("tp")
    zh, x = s // 4, lax.rem(s, 4)
    zl, y, c = t // 8, lax.rem(t // 2, 4), lax.rem(t, 2)
    oz, oc, oh = 1 - zl, 1 - c, 1 - zh
    yp, ym, y2 = lax.rem(y + 1, 4), lax.rem(y + 3, 4), lax.rem(y + 2, 4)
    xp, xm, x2 = lax.rem(x + 1, 4), lax.rem(x + 3, 4), lax.rem(x + 2, 4)

    def dev(zh_=zh, x_=x, zl_=zl, y_=y, c_=c):
        return (zh_ * 4 + x_, zl_ * 8 + y_ * 2 + c_)

    XP, XM, X2 = dev(x_=xp), dev(x_=xm), dev(x_=x2)
    YP, YM = dev(y_=yp), dev(y_=ym)
    ZL, ZH, CO = dev(zl_=oz), dev(zh_=oh), dev(c_=oc)

    copies = {}

    def send(name, k, src, dst, to):
        i = SEM[(name, k)]
        cp = pltpu.make_async_remote_copy(
            src_ref=src, dst_ref=dst, send_sem=ssem.at[i], recv_sem=rsem.at[i],
            device_id=to, device_id_type=MESH,
        )
        cp.start()
        copies[(name, k)] = cp

    def recv(k, *names):
        for name in names:
            copies[(name, k)].wait_recv()

    local = []

    def local_copy(src, dst):
        cp = pltpu.make_async_copy(src, dst, lsem.at[len(local)])
        cp.start()
        local.append(cp)
        return cp

    def src_of(k):
        return k // NP

    def hid_of(k):
        return pl.ds(BASES[k % NP], PARTS[k % NP])

    def sizes(k):
        h, w = PARTS[k % NP], YCOLS[k]
        return h, w, 3 * h - w, (3 * h - w) // 2

    def all_cols(k):
        return pl.ds(3 * BASES[k % NP], 3 * PARTS[k % NP])

    def y_cols(k):
        return pl.ds(3 * BASES[k % NP], ACOLS[k])

    def z_cols(k):
        return pl.ds(3 * BASES[k % NP] + ACOLS[k], 3 * PARTS[k % NP] - ACOLS[k])

    def z_half(k, half):
        width = (3 * PARTS[k % NP] - ACOLS[k]) // 2
        return pl.ds(3 * BASES[k % NP] + ACOLS[k] + half * width, width)

    barrier = pltpu.get_barrier_semaphore()
    peers = [XP, XM, YP, YM, ZL, ZH, CO, X2]
    for peer in peers:
        pl.semaphore_signal(barrier, inc=1, device_id=peer, device_id_type=MESH)
    raw = [local_copy(acts_hbm, acts_ref), local_copy(grads_hbm, grads_ref)]
    loads = [local_copy(gate_hbm, wg), local_copy(up_hbm, wu), local_copy(down_hbm, wd)]
    hot, weight = routing(lengths_ref[...], dest_ref[...], adv_ref[...], mask_ref[...])

    def spread_own(arr, n):
        send("zh" + n, 0, G.at[arr, 0, zh], G.at[arr, 0, zh], ZH)
        send("xo" + n + "+", 0, G.at[arr, 0, zh], G.at[arr, 1, zh], XP)
        send("xo" + n + "-", 0, G.at[arr, 0, zh], G.at[arr, 2, zh], XM)

    def spread_peer(arr, n):
        recv(0, "zh" + n)
        send("q" + n, 0, G.at[arr, 0, oc], Q.at[arr, 0], CO)
        send("xp" + n + "+", 0, G.at[arr, 0, oh], G.at[arr, 1, oh], XP)
        send("xp" + n + "-", 0, G.at[arr, 0, oh], G.at[arr, 2, oh], XM)

    def pack_acts(k):
        raw[0].wait()
        G[0, 0, zh] = jnp.dot(hot, acts_ref[...], preferred_element_type=F32).astype(BF)
        pl.semaphore_wait(barrier, len(peers))
        spread_own(0, "a")

    def pack_grads(k):
        raw[1].wait()
        packed = jnp.dot(hot, grads_ref[...], preferred_element_type=F32)
        G[1, 0, zh] = (packed * weight).astype(BF)
        spread_own(1, "g")

    def swap_weights(k):
        for cp in loads:
            cp.wait()
        for j in range(NP):
            hid = hid_of(j)
            send("wg", j, wg.at[:, hid], pg.at[:, hid], CO)
            send("wu", j, wu.at[:, hid], pu.at[:, hid], CO)
            send("wd", j, wd.at[hid], pd.at[hid], CO)

    def peer_acts(k):
        spread_peer(0, "a")

    def peer_grads(k):
        spread_peer(1, "g")

    def pass_on(k):
        recv(0, "xoa+", "xpa+", "xoa-", "xpa-", "xog+", "xpg+", "xog-", "xpg-")
        send("xf+", 0, G.at[:, 1, 0], G.at[:, 3, 0], XP)
        send("xf-", 0, G.at[:, 2, 1], G.at[:, 3, 1], XM)
        for n in (1, 2):
            send("qa", n, G.at[0, n, oc], Q.at[0, n], CO)
            send("qg", n, G.at[1, n, oc], Q.at[1, n], CO)

    def far_rows(k):
        recv(0, "xf+", "xf-")
        send("qa", 3, G.at[0, 3, oc], Q.at[0, 3], CO)
        send("qg", 3, G.at[1, 3, oc], Q.at[1, 3], CO)

    Y_ORDER = ((0, y2), (1, y2), (1, yp), (0, ym), (0, yp), (1, ym), (0, y), (1, y))
    Z_ORDER = tuple((oz, n) for n in range(4)) + tuple((zl, n) for n in range(4))

    def rows_in(ref, index, order):
        return jnp.concatenate(
            [ref[index + (pl.ds(pl.multiple_of((a * 4 + b) * BIN, BIN), BIN),)] for a, b in order], axis=0
        )

    def keep(raw, full, k, first, part):
        width = part.shape[1]
        raw[k, :, :, first:first + width] = part[:64].astype(BF).reshape(4, BIN, width)
        full[k, :, :, first:first + width] = part[64:].reshape(4, BIN, width)

    def product(a, b, own, par):
        return jnp.dot(a, own, preferred_element_type=F32) + jnp.dot(b, par, preferred_element_type=F32)

    def forward_y(k):
        n, j = src_of(k), k % NP
        h, w, _, _ = sizes(k)
        base = BASES[j]
        recv(n, "qa") if j == 0 else None
        recv(j, "wg", "wu") if n == 0 else None
        a, b = rows_in(G, (0, n, c), Y_ORDER), rows_in(Q, (0, n), Y_ORDER)
        cols = slice(base, base + h)
        keep(RY, FY, k, 0, product(a, b, wg[:, cols], pg[:, cols]))
        if w > h:
            cols = slice(base, base + w - h)
            keep(RY, FY, k, h, product(a, b, wu[:, cols], pu[:, cols]))
        send("y1+", k, RY.at[k, 0, :, pl.ds(0, w)], y1.at[k, 0, :, pl.ds(0, w)], YP)
        send("y1-", k, RY.at[k, 1, :, pl.ds(0, w)], y1.at[k, 1, :, pl.ds(0, w)], YM)
        send("yo+", k, RY.at[k, 2, :, pl.ds(0, w)], yown.at[k, 1, :, pl.ds(0, w)], YP)
        send("yo-", k, RY.at[k, 3, :, pl.ds(0, w)], yown.at[k, 0, :, pl.ds(0, w)], YM)

    def forward_z(k):
        n, j = src_of(k), k % NP
        h, w, v, _ = sizes(k)
        base = BASES[j]
        a, b = rows_in(G, (0, n, c), Z_ORDER), rows_in(Q, (0, n), Z_ORDER)
        cols = slice(base + w - h, base + h)
        keep(RZ, FZ, k, 0, product(a, b, wu[:, cols], pu[:, cols]))
        recv(n, "qg") if j == 0 else None
        recv(j, "wd") if n == 0 else None
        a, b = rows_in(G, (1, n, c), Z_ORDER), rows_in(Q, (1, n), Z_ORDER)
        part = lax.dot_general(a, wd[base:base + h, :], NT, preferred_element_type=F32)
        part += lax.dot_general(b, pd[base:base + h, :], NT, preferred_element_type=F32)
        keep(RZ, FZ, k, 2 * h - w, part)
        send("z1", k, RZ.at[k, :, :, pl.ds(0, v)], z1.at[k, :, :, pl.ds(0, v)], ZL)

    def pass_y(k, half, name, to):
        w = sizes(k)[1]
        recv(k, "y1" + name)
        y1[k, half, :, :w] = (up32(y1[k, half, :, :w]) + FY[k, half, :, :w]).astype(BF)
        send("ya" + name, k, y1.at[k, half, :, pl.ds(0, w)], yacc.at[k, half, :, pl.ds(0, w)], to)

    def plus_y(k):
        pass_y(k, 0, "+", YP)

    def minus_y(k):
        pass_y(k, 1, "-", YM)

    def pass_z(k):
        _, _, v, u = sizes(k)
        recv(k, "z1")
        for row in (y2, yp, ym):
            z1[k, row, :, :v] = (up32(z1[k, row, :, :v]) + FZ[k, row, :, :v]).astype(BF)
        low, high = pl.ds(0, u), pl.ds(u, u)
        send("r1+", k, z1.at[k, y2, :, low], r1.at[k, 0, :, low], YP)
        send("r1-", k, z1.at[k, y2, :, high], r1.at[k, 1, :, low], YM)
        send("ro+", k, z1.at[k, yp, :, high], rown.at[k, 1, :, low], YP)
        send("ro-", k, z1.at[k, ym, :, low], rown.at[k, 0, :, low], YM)

    def cross_z(k):
        w = sizes(k)[1]
        recv(k, "yo+", "yo-", "ya+", "ya-")
        total = FY[k, 2 + oz, :, :w] + up32(yacc[k, oz, :, :w]) + up32(yown[k, oz, :, :w])
        ysend[k, :, :w] = total.astype(BF)
        send("yz", k, ysend.at[k, :, pl.ds(0, w)], yz.at[k, :, pl.ds(0, w)], ZL)

    def pass_r(k, half, name, row, to):
        u = sizes(k)[3]
        recv(k, "r1" + name)
        total = up32(r1[k, half, :, :u]) + up32(z1[k, row, :, half * u:half * u + u])
        r1[k, half, :, :u] = total.astype(BF)
        send("ra" + name, k, r1.at[k, half, :, pl.ds(0, u)], racc.at[k, half, :, pl.ds(0, u)], to)

    def plus_r(k):
        pass_r(k, 0, "+", yp, YP)

    def minus_r(k):
        pass_r(k, 1, "-", ym, YM)

    def finish(k):
        n = src_of(k)
        h, w, v, u = sizes(k)
        base = 3 * BASES[k % NP]
        recv(k, "yz", "ro+", "ro-", "ra+", "ra-")
        mine = zl * 4 + y
        F[:, :w] = (
            FY[k, 2 + zl, :, :w] + up32(yacc[k, zl, :, :w]) + up32(yown[k, zl, :, :w]) + up32(yz[k, :, :w])
        )
        for half in (0, 1):
            cols = slice(half * u, half * u + u)
            F[:, w + half * u:w + half * u + u] = (
                FZ[k, y, :, cols] + up32(z1[k, y, :, cols])
                + up32(racc[k, half, :, :u]) + up32(rown[k, half, :, :u])
            )
        gate, upper, back = F[:, :h], F[:, h:2 * h], F[:, 2 * h:3 * h]
        sigma = jax.nn.sigmoid(gate)
        swish = gate * sigma
        H[n, c, mine, :, base:base + h] = (swish * upper).astype(BF)
        H[n, c, mine, :, base + h:base + 2 * h] = (
            back * upper * sigma * (1.0 + gate * (1.0 - sigma))
        ).astype(BF)
        H[n, c, mine, :, base + 2 * h:base + 3 * h] = (back * swish).astype(BF)
        a = H.at[n, c, mine, :, y_cols(k)]
        b = H.at[n, c, mine, :, z_cols(k)]
        send("az", k, a, a, ZL)
        send("ay+", k, a, a, YP)
        send("ay-", k, a, a, YM)
        send("by+", k, b, b, YP)
        send("by-", k, b, b, YM)
        send("bz0", k, b, b, ZL)

    def move(name, k, plane, row, cols, to):
        part = H.at[src_of(k), c, plane * 4 + row, :, cols]
        send(name, k, part, part, to)

    def plus_b(k):
        recv(k, "by+")
        move("bf+", k, zl, ym, z_half(k, 0), YP)
        move("bz1", k, zl, ym, z_cols(k), ZL)

    def minus_b(k):
        recv(k, "by-")
        move("bf-", k, zl, yp, z_half(k, 1), YM)
        move("bz2", k, zl, yp, z_cols(k), ZL)

    def plane_a(k):
        recv(k, "az")
        move("ap+", k, oz, y, y_cols(k), YP)
        move("ap-", k, oz, y, y_cols(k), YM)

    def plus_a(k):
        recv(k, "ay+")
        move("af+", k, zl, ym, y_cols(k), YP)

    def far_b(k):
        recv(k, "bf+", "bf-")
        move("bz3", k, zl, y2, z_cols(k), ZL)

    def far_a(k):
        recv(k, "ap-")
        move("af-", k, oz, yp, y_cols(k), YM)

    def core_near(k):
        recv(k, "ay-")
        for n, row in enumerate((y, ym, yp)):
            move(f"ca{n}", k, zl, row, all_cols(k), CO)

    def core_far(k):
        recv(k, "af+", "af-", "ap+", "bz0", "bz1", "bz2", "bz3")
        part = H.at[src_of(k), c, pl.ds(oz * 4, 4), :, all_cols(k)]
        send("cc0", k, part, part, CO)
        move("cc1", k, zl, y2, all_cols(k), CO)

    def outputs(k):
        n, j = src_of(k), k % NP
        h = sizes(k)[0]
        base = 3 * BASES[j]
        hid = slice(BASES[j], BASES[j] + h)
        recv(k, "ca0", "ca1", "ca2", "cc0", "cc1")
        shape = (2, 2, 4, BIN, WIDTH)
        first = H[n, :, :, :, base:base + h].reshape(256, h)
        block = jnp.dot(first, wd[hid, :], preferred_element_type=F32).reshape(shape)
        if j > 0:
            block += OB[n, :, :, :, :, :WIDTH]
        OB[n, :, :, :, :, :WIDTH] = block
        if j == NP - 1:
            OL[n, :, :, :, :, :WIDTH] = block.astype(BF)
            if n == NS - 1:
                late_sends(0)
        first = H[n, :, :, :, base + h:base + 2 * h].reshape(256, h)
        inner = lax.dot_general(first, wg[:, hid], NT, preferred_element_type=F32)
        first = H[n, :, :, :, base + 2 * h:base + 3 * h].reshape(256, h)
        inner += lax.dot_general(first, wu[:, hid], NT, preferred_element_type=F32)
        inner = inner.reshape(shape)
        if j > 0:
            inner += OB[n, :, :, :, :, WIDTH:]
        OB[n, :, :, :, :, WIDTH:] = inner
        if j < NP - 1:
            return
        OL[n, :, :, :, :, WIDTH:] = inner.astype(BF)
        if n < NS - 1:
            send("m+", n, OL.at[n, :, :, xp], rm.at[n], XP)
            send("m-", n, OL.at[n, :, :, xm], rp.at[n], XM)
            send("m2", n, OL.at[n, :, :, x2], r2.at[n], X2)
        else:
            late_sends(1)

    def late_sends(side):
        cols = pl.ds(side * WIDTH, WIDTH)
        for name, slot, a, b in (
            ("dzx2", 6, oh, x2), ("dzx+", 4, oh, xp), ("dzx-", 5, oh, xm), ("dz", 3, oh, x),
            ("dx2", 2, zh, x2), ("dx+", 0, zh, xp), ("dx-", 1, zh, xm),
        ):
            send(name, side, OL.at[NS - 1, :, a, b, :, cols], dr.at[slot, :, :, cols], dev(zh_=a, x_=b))

    PLACES = ((0, 2, 1, 3), (2, 3, 0, 1), (3, 1, 2, 0), (1, 0, 3, 2))

    def earlier_sum(r, half):
        total = None
        for n, ref in zip(PLACES[r], (None, rm, rp, r2)):
            if n < NS - 1:
                part = OB[n, :, half, x] if ref is None else up32(ref[n, :, half])
                total = part if total is None else total + part
        return total

    def seq_exchange(k):
        for n in range(NS - 1):
            recv(n, "m+", "m-", "m2")
        for r in range(4):
            sz[r] = earlier_sum(r, oh).astype(BF)
        send("sz", 0, sz, rz, ZH)

    def seq_finish(k):
        recv(0, "sz")
        for side in (0, 1):
            recv(side, *LATE_NAMES)
        late = {0: (2, 6), 1: (0, 4), 2: (3,), 3: (1, 5)}
        for r in range(4):
            total = earlier_sum(r, zh) + up32(rz[r])
            for j in late[r]:
                total += up32(dr[j])
            if r == 2:
                total += OB[NS - 1, :, zh, x]
            total = total.astype(BF)
            source = lax.rem(x + r, 4)
            block_out[:, source] = total[:, :, :WIDTH]
            input_out[:, source] = total[:, :, WIDTH:]

    def weight_grads(k):
        acts = G[0].reshape(1024, WIDTH)
        grads = G[1].reshape(1024, WIDTH)
        for j in range(NP):
            h = PARTS[j]
            for at in range(0, h, 512):
                width = min(512, h - at)
                to = pl.ds(BASES[j] + at, width)
                for place, out in ((1, tg), (2, tu)):
                    cols = pl.ds(3 * BASES[j] + place * h + at, width)
                    part = H[:, :, :, :, cols].reshape(1024, width)
                    part = lax.dot_general(acts, part, TN, preferred_element_type=F32)
                    out[:, to] = (part * (1.0 / 32.0)).astype(BF)
                part = H[:, :, :, :, pl.ds(3 * BASES[j] + at, width)].reshape(1024, width)
                part = lax.dot_general(part, grads, TN, preferred_element_type=F32)
                td[to, :] = (part * (1.0 / 32.0)).astype(BF)

    steps = (
        pack_acts, pack_grads, swap_weights, peer_acts, peer_grads, pass_on, far_rows,
        forward_y, forward_z, plus_y, minus_y, pass_z, cross_z, plus_r, minus_r, finish,
        plus_b, minus_b, plane_a, plus_a, far_b, far_a, core_near, core_far, outputs,
        seq_exchange, weight_grads, seq_finish,
    )
    for step in ORDER:
        steps[step // 10](step % 10)
    for cp in copies.values():
        cp.wait_send()


def run_mega(acts, grads, lengths, dest, mask, adv, gate, up, down):
    vm = pltpu.VMEM
    shape = jax.ShapeDtypeStruct
    rows = vm((2, 4, BIN, WIDTH), BF)
    wide, tall = vm((WIDTH, HID), BF), vm((HID, WIDTH), BF)
    hbm = pl.BlockSpec(memory_space=pl.ANY)
    whole = pl.BlockSpec(memory_space=vm)
    late = vm((NS - 1, 2, 2, BIN, 2 * WIDTH), BF)
    ybuf, zbuf = vm((NK, 2, BIN, MAXY), BF), vm((NK, 2, BIN, MAXZ // 2), BF)
    return pl.pallas_call(
        mega,
        out_shape=(rows, rows, wide, wide, tall),
        in_specs=[hbm] * 2 + [whole] * 4 + [hbm] * 3,
        out_specs=(whole,) * 5,
        scratch_shapes=[
            vm((2 * 128, WIDTH), BF), vm((2 * 128, WIDTH), BF),
            vm((WIDTH, HID), BF), vm((WIDTH, HID), BF), vm((HID, WIDTH), BF),
            vm((WIDTH, HID), BF), vm((WIDTH, HID), BF), vm((HID, WIDTH), BF),
            vm((2, NS, 2, 128, WIDTH), BF),
            vm((2, NS, 128, WIDTH), BF),
            vm((NK, 4, BIN, MAXY), BF), vm((NK, 4, BIN, MAXZ), BF),
            vm((NK, 4, BIN, MAXY), F32), vm((NK, 4, BIN, MAXZ), F32),
            vm((NS, 2, 8, BIN, ALL), BF),
            ybuf, ybuf, ybuf,
            vm((NK, BIN, MAXY), BF), vm((NK, BIN, MAXY), BF),
            vm((NK, 4, BIN, MAXZ), BF),
            zbuf, zbuf, zbuf,
            vm((BIN, 3 * max(PARTS)), F32),
            vm((NS, 2, 2, 4, BIN, 2 * WIDTH), F32),
            vm((NS, 2, 2, 4, BIN, 2 * WIDTH), BF),
            late, late, late,
            vm((4, 2, BIN, 2 * WIDTH), BF), vm((4, 2, BIN, 2 * WIDTH), BF),
            vm((7, 2, BIN, 2 * WIDTH), BF),
            pltpu.SemaphoreType.DMA((N_SEM,)),
            pltpu.SemaphoreType.DMA((N_SEM,)),
            pltpu.SemaphoreType.DMA((8,)),
        ],
        compiler_params=pltpu.CompilerParams(
            collective_id=0, has_side_effects=True, vmem_limit_bytes=54 * 2**20
        ),
        name="mega",
    )(acts, grads, lengths, dest, mask, adv, gate, up, down)


def widen_kernel(
    block, inner, wide_a, wide_b, tall, out_block, out_inner, out_a, out_b, out_c, stage, stage_tall, sem
):
    small = [
        pltpu.make_async_copy(block, out_block, sem.at[4]), pltpu.make_async_copy(inner, out_inner, sem.at[5])
    ]
    for cp in small:
        cp.start()
    pieces = [(src, dst, at, 128, stage) for src, dst in ((wide_a, out_a), (wide_b, out_b)) for at in range(0, WIDTH, 128)]
    pieces += [(tall, out_c, at, 480, stage_tall) for at in range(0, HID, 480)]
    flying = []
    for n, (src, dst, at, rows, held) in enumerate(pieces):
        slot = n % 4
        if n >= 4:
            flying[n - 4].wait()
        held[slot] = up32(src[at:at + rows, :])
        cp = pltpu.make_async_copy(held.at[slot], dst.at[pl.ds(at, rows)], sem.at[slot])
        cp.start()
        flying.append(cp)
    for cp in flying[-4:] + small:
        cp.wait()


def widen(block, inner, wide_a, wide_b, tall):
    shape = jax.ShapeDtypeStruct
    return pl.pallas_call(
        widen_kernel,
        out_shape=(
            shape(block.shape, BF), shape(inner.shape, BF),
            shape((WIDTH, HID), F32), shape((WIDTH, HID), F32), shape((HID, WIDTH), F32),
        ),
        in_specs=[pl.BlockSpec(memory_space=pltpu.VMEM)] * 5,
        out_specs=(pl.BlockSpec(memory_space=pl.ANY),) * 5,
        scratch_shapes=[
            pltpu.VMEM((4, 128, HID), F32), pltpu.VMEM((4, 480, WIDTH), F32), pltpu.SemaphoreType.DMA((6,)),
        ],
        compiler_params=pltpu.CompilerParams(vmem_limit_bytes=12 * 2**20),
        name="widen",
    )(block, inner, wide_a, wide_b, tall)


def per_device(
    rollout_acts, rollout_grads, lengths, destination, valid_mask, advantage,
    gate_weight, up_weight, down_weight,
):
    block, inner, gate_grad, up_grad, down_grad = run_mega(
        rollout_acts, rollout_grads, lengths, destination, valid_mask[None, :], advantage,
        gate_weight, up_weight, down_weight,
    )
    return widen(block.reshape(128, WIDTH), inner.reshape(128, WIDTH), gate_grad, up_grad, down_grad)


def solution(mesh):
    return jax.shard_map(
        per_device,
        mesh=mesh,
        in_specs=(
            P("seq", "tp"), P("seq", "tp"), P("seq", None), P("seq", None), P("seq"),
            P("seq", None), P("tp", "seq"), P("tp", "seq"), P("seq", "tp"),
        ),
        out_specs=(P("seq", "tp"), P("seq", "tp"), P("tp", "seq"), P("tp", "seq"), P("seq", "tp")),
        check_vma=False,
    )
```
